256 devices in a mesh: dp: 16 (over y, x), sx: 16 (over z, core).
Axes of the slice: x: 4, y: 4, z: 8, core: 2. Of those that a mesh axis runs over, the one named last changes fastest.
Arguments:
- hidden: bfloat16 [32768, 3200], P(('dp', 'sx')), parts along dimension 0, may hold values from -6 to 6
- norm_gain: bfloat16 [3200], replicated, may hold values from 0.5 to 1.5
- route_expert: int32 [32768, 1], P(('dp', 'sx')), parts along dimension 0, may hold values from 0 to 15, as said below
- route_weight: float32 [32768], P(('dp', 'sx')), parts along dimension 0, may hold values from 0.3 to 1
- priority: int32 [32768], P(('dp', 'sx')), parts along dimension 0, may hold values from 0 to 2047, each once
- expert_gate_up: bfloat16 [3200, 2, 10240], P(None, None, 'sx'), may hold values from -0.109375 to 0.109375
- expert_down: bfloat16 [10240, 3200], P('sx'), may hold values from -0.0625 to 0.0625
Outputs:
- layer_out: bfloat16 [32768, 3200], P(('dp', 'sx')), parts along dimension 0
The draws below stay inside these ranges and needn't reach their ends.
There are 16 independent parts, one for each index of `dp`. The reference program is written for one: setup_inputs(seed, part) draws one part's arguments, and reference() takes and returns one part's arrays. A program takes and returns all parts, laid end to end along the dimension named above; an argument that names none is the same for every part. Nothing has to cross between parts.
Inputs may be any that keep to these rules, and one draw needn't show every extreme that they name: `route_expert`: in the rows of one device at most 64 tokens name expert 0, and in every draw some device's rows name it exactly 64 times.
All inputs are finite; a program needn't handle non-finite values.
Results may differ from the reference program's by a relative error of at most 0.007.
Values may be sent and summed in bfloat16 or wider, within the bound.
No kernel may reach another device: no remote copies, remote signals or barrier semaphores. Data moves between devices by JAX's collectives and lax.ppermute only.
A program may use at most 128 MiB of HBM per device.

```python
import jax
import jax.numpy as jnp
from jax import lax

D = 3200
FR = 10240
EXPERTS = 16
TOK_DEV = 128
M = 64
NEW_TOK = 2048
CAP = 384
N_SX = 16


def draw_route_expert(key, part):
    key = jax.random.fold_in(key, 7)
    keys = jax.random.split(key, 4)
    counts = jax.random.randint(keys[0], (N_SX,), M // 2, M + 1)
    fullest = jax.random.randint(keys[1], (), 0, N_SX)
    counts = jnp.where(jnp.arange(N_SX) == fullest, M, counts)
    scores = jax.random.randint(keys[2], (N_SX, TOK_DEV), 0, 1048576) * TOK_DEV + jnp.arange(TOK_DEV)[None, :]
    places = jnp.argsort(jnp.argsort(scores, axis=1), axis=1)
    others = jax.random.randint(keys[3], (N_SX, TOK_DEV), 1, EXPERTS)
    chosen = jnp.where(places < counts[:, None], 0, others)
    return chosen.reshape(N_SX * TOK_DEV, 1).astype(jnp.int32)


def block_scale(key, extent, cuts, smallest, top_value):
    loudness, own = 1.0, jax.random.fold_in(key, 6)
    for dim, shards_of in cuts:
        heights = jnp.exp(jax.random.uniform(jax.random.fold_in(own, dim), (shards_of,), jnp.float32, smallest / len(cuts), top_value / len(cuts)))
        loudness = loudness * jnp.repeat(heights, extent[dim] // shards_of).reshape([-1 if axis == dim else 1 for axis in range(len(extent))])
    return loudness


def gaussian(key, shape, spread, reach, cuts=(), kind=jnp.bfloat16):
    entries = spread * jax.random.normal(key, shape, jnp.float32)
    if cuts:
        entries = entries * block_scale(key, shape, cuts, -0.22, 0.18)
    return jnp.clip(entries, -reach, reach).astype(kind)


def setup_inputs(seed: int = 0, part: int = 0) -> dict:
    splits = jax.random.split(jax.random.key(seed), 8)
    part_splits = jax.random.split(jax.random.fold_in(splits[7], part), 8)
    return {
        "hidden": gaussian(part_splits[0], (NEW_TOK, D), 1.0, 6.0, ((0, 16),)),
        "norm_gain": jnp.clip(1.0 + 0.1 * jax.random.normal(splits[1], (D,), jnp.float32), 0.5, 1.5).astype(jnp.bfloat16),
        "route_expert": draw_route_expert(jax.random.fold_in(jax.random.fold_in(splits[7], part), 71), part),
        "route_weight": jnp.clip(0.3 + 0.7 * jax.random.uniform(part_splits[3], (NEW_TOK,), jnp.float32) ** block_scale(part_splits[3], (NEW_TOK,), ((0, 16),), -0.2, 0.2), 0.3, 1.0),
        "priority": jax.random.permutation(part_splits[4], NEW_TOK).astype(jnp.int32),
        "expert_gate_up": gaussian(splits[5], (D, 2, FR), D ** -0.5, 0.109375, ((2, 16),)),
        "expert_down": gaussian(splits[6], (FR, D), FR ** -0.5, 0.0625, ((0, 16),)),
    }


def reference(hidden, norm_gain, route_expert, route_weight, priority, expert_gate_up, expert_down):
    resid_float = hidden.astype(jnp.float32)
    scale_rows = lax.rsqrt(lax.optimization_barrier(jnp.mean(resid_float * resid_float, axis=1, keepdims=True)) + 1e-06)
    normed = (resid_float * scale_rows * norm_gain.astype(jnp.float32)[None, :]).astype(jnp.bfloat16)
    flight = route_expert[:, 0] == 0
    earlier = (priority[None, :] < priority[:, None]) & flight[None, :]
    rank_all = lax.optimization_barrier(jnp.sum(earlier.astype(jnp.int32), axis=1))
    kept_rows = flight & (rank_all < CAP)
    token_index = jnp.arange(NEW_TOK, dtype=jnp.int32)
    match = kept_rows[None, :] & (rank_all[None, :] == jnp.arange(CAP, dtype=jnp.int32)[:, None])
    slot_tokens = lax.optimization_barrier(jnp.sum(jnp.where(match, token_index[None, :], 0), axis=1)).astype(jnp.int32)
    expert_in = jnp.take(normed, slot_tokens, axis=0)
    units_all = jnp.dot(expert_in, expert_gate_up.reshape(D, 2 * FR), preferred_element_type=jnp.float32)
    activation = (jax.nn.silu(units_all[:, :FR]) * units_all[:, FR:]).astype(jnp.bfloat16)
    slot_out = jnp.dot(activation, expert_down, preferred_element_type=jnp.float32).astype(jnp.bfloat16)
    slot_out = lax.optimization_barrier(slot_out).astype(jnp.float32)
    routed = jnp.take(slot_out, jnp.clip(rank_all, 0, CAP - 1).astype(jnp.int32), axis=0)
    routed = jnp.where(kept_rows[:, None], routed, jnp.float32(0.0))
    total = resid_float + route_weight[:, None] * routed
    return total.astype(jnp.bfloat16)
```

```python
import jax
import jax.numpy as jnp
from jax import lax
from jax.sharding import PartitionSpec as P

ROW_SCALE = 256.0
NO_TOKEN = 4096.0
LANES = 128


def expert_rows(rows, expert_gate_up, expert_down, count, chunk):
    devices, _, _ = rows.shape
    features, _, fr_dev = expert_gate_up.shape
    used = rows[:, :count, :features].reshape(devices * count, features)
    normed = (used.astype(jnp.float32) * (1.0 / ROW_SCALE)).astype(jnp.bfloat16)
    units = jnp.einsum("td,dgf->gtf", normed, expert_gate_up, preferred_element_type=jnp.float32)
    hidden = (jax.nn.silu(units[0]) * units[1]).astype(jnp.bfloat16).reshape(devices, count, fr_dev)
    if chunk <= count:
        hidden = hidden[:, :chunk]
    else:
        hidden = jnp.pad(hidden, ((0, 0), (0, chunk - count), (0, 0)))
    share = jnp.dot(
        hidden.reshape(devices * chunk, fr_dev), expert_down, preferred_element_type=jnp.float32
    ).astype(jnp.bfloat16)
    return lax.psum_scatter(share, "sx", scatter_dimension=0, tiled=True)


def on_device(hidden, norm_gain, route_expert, route_weight, priority, expert_gate_up, expert_down):
    devices = lax.axis_size("sx")
    tok_dev, features = hidden.shape
    slot_count = tok_dev // 2
    cap_rows = 3 * slot_count * devices // 8
    resid_float = hidden.astype(jnp.float32)
    scale_rows = lax.rsqrt(jnp.mean(resid_float * resid_float, axis=1, keepdims=True) + 1e-06)
    normed = (resid_float * scale_rows * norm_gain.astype(jnp.float32)[None, :]).astype(
        jnp.bfloat16
    )
    flight = route_expert[:, 0] == 0
    ahead = flight[None, :] & (priority[None, :] < priority[:, None])
    slot = jnp.sum(ahead.astype(jnp.int32), axis=1)
    selected = (jnp.arange(slot_count, dtype=jnp.int32)[:, None] == slot[None, :]) & flight[None, :]
    packed = jnp.dot(selected.astype(jnp.bfloat16), normed, preferred_element_type=jnp.float32)
    slot_priority = jnp.sum(
        jnp.where(selected, priority.astype(jnp.float32)[None, :] - NO_TOKEN, 0.0), axis=1
    )
    sent = jnp.concatenate(
        [
            (packed * ROW_SCALE).astype(jnp.float16),
            jnp.broadcast_to(
                (slot_priority + NO_TOKEN).astype(jnp.float16)[:, None], (slot_count, LANES)
            ),
        ],
        axis=1,
    )
    gathered = lax.all_gather(sent, "sx", axis=0, tiled=True)
    ranked = gathered[:, features].astype(jnp.float32)
    rank = jnp.sum((ranked[None, :] < ranked[:, None]).astype(jnp.int32), axis=1)
    kept = (ranked < NO_TOKEN) & (rank < cap_rows)
    kept_counts = jnp.sum(kept.reshape(devices, slot_count).astype(jnp.int32), axis=1)
    own_count = lax.dynamic_index_in_dim(kept_counts, lax.axis_index("sx"), keepdims=False)
    kept_local = flight & (slot < own_count)
    rows = gathered.reshape(devices, slot_count, features + LANES)

    def finish(returned):
        place = (
            (jnp.arange(returned.shape[0], dtype=jnp.int32)[None, :] == slot[:, None])
            & kept_local[:, None]
        ).astype(jnp.bfloat16)
        routed = jnp.dot(place, returned, preferred_element_type=jnp.float32)
        return (resid_float + route_weight[:, None] * routed).astype(jnp.bfloat16)

    few = 3 * slot_count // 4

    def narrow(rows):
        return finish(expert_rows(rows, expert_gate_up, expert_down, few, few - 1))

    def wide(rows):
        return finish(
            expert_rows(rows, expert_gate_up, expert_down, slot_count, slot_count + 15)
        )

    return lax.cond(jnp.max(kept_counts) < few, narrow, wide, rows)


def solution(mesh):
    in_specs = (
        P(("dp", "sx"), None),
        P(),
        P(("dp", "sx"), None),
        P(("dp", "sx")),
        P(("dp", "sx")),
        P(None, None, "sx"),
        P("sx", None),
    )
    out_specs = P(("dp", "sx"), None)
    return jax.shard_map(
        on_device, mesh=mesh, in_specs=in_specs, out_specs=out_specs, check_vma=False
    )
```

```python
import functools

import jax
import jax.numpy as jnp
from jax import lax
from jax.experimental import pallas as pl
from jax.experimental.pallas import tpu as pltpu
from jax.sharding import PartitionSpec as P

ROW_SCALE = 256.0
NO_TOKEN = 4096
RADIX = 64
LANES = 128
COLUMNS = 1280
VMEM = pltpu.VMEM


def as_column(row):
    n = row.shape[1]
    square = lax.broadcasted_iota(jnp.int32, (n, n), 0) == lax.broadcasted_iota(
        jnp.int32, (n, n), 1
    )
    return jnp.sum(jnp.where(square, row, jnp.zeros_like(row)), axis=1, keepdims=True)


def pack_kernel(
    hidden_ref, gain_ref, expert_ref, priority_ref, weight_ref,
    first_ref, all_ref, slot_ref, asked_ref, scale_ref,
):
    slots = all_ref.shape[0]
    few = first_ref.shape[0]
    tokens = hidden_ref.shape[0]
    flight = (expert_ref[...] == 0).astype(jnp.float32)
    priority = priority_ref[...].astype(jnp.float32)
    own = jnp.where(flight > 0, priority, float(NO_TOKEN))
    own_column = as_column(own)
    slot_row = jnp.sum((own_column < own).astype(jnp.float32), axis=0, keepdims=True)
    slot_column = jnp.sum((own < own_column).astype(jnp.float32), axis=1, keepdims=True)
    slot_row = jnp.where(flight > 0, slot_row, float(slots))
    slot_column = jnp.where(own_column < NO_TOKEN, slot_column, float(slots))
    slot_ref[...] = slot_row.astype(jnp.int32)
    asked_ref[...] = own_column
    scale_ref[...] = as_column(weight_ref[...])

    resid = hidden_ref[...].astype(jnp.float32)
    scale = lax.rsqrt(jnp.mean(resid * resid, axis=1, keepdims=True) + 1e-06)
    normed = (resid * scale * gain_ref[...].astype(jnp.float32)).astype(jnp.bfloat16)
    place = lax.broadcasted_iota(jnp.int32, (slots, tokens), 0).astype(jnp.float32) == slot_row
    selector = jnp.where(place, ROW_SCALE, 0.0).astype(jnp.bfloat16)
    packed = jnp.dot(selector, normed, preferred_element_type=jnp.float32)
    all_ref[...] = packed.astype(jnp.bfloat16)

    lane = lax.broadcasted_iota(jnp.int32, (tokens, LANES), 1)
    holds = lax.rem(lane, slots).astype(jnp.float32) == slot_column
    held = NO_TOKEN + jnp.sum(
        jnp.where(holds, own_column - NO_TOKEN, 0.0), axis=0, keepdims=True
    )
    quotient = jnp.floor(held * (1.0 / RADIX))
    low = lax.broadcasted_iota(jnp.int32, (1, LANES), 1) < slots
    code = jnp.where(low, quotient, held - quotient * RADIX)
    row = lax.broadcasted_iota(jnp.int32, (few, LANES), 0)
    first_ref[:, LANES:] = packed[:few, LANES:].astype(jnp.bfloat16)
    first_ref[:, :LANES] = jnp.where(row == few - 1, code, packed[:few, :LANES]).astype(
        jnp.bfloat16
    )


def pack(hidden, norm_gain, route_expert, priority, route_weight):
    tokens, features = hidden.shape
    slots = tokens // 2
    few = 3 * slots // 4
    return pl.pallas_call(
        pack_kernel,
        out_shape=(
            jax.ShapeDtypeStruct((few, features), jnp.bfloat16),
            jax.ShapeDtypeStruct((slots, features), jnp.bfloat16),
            jax.ShapeDtypeStruct((1, tokens), jnp.int32),
            jax.ShapeDtypeStruct((tokens, 1), jnp.float32),
            jax.ShapeDtypeStruct((tokens, 1), jnp.float32),
        ),
        compiler_params=pltpu.CompilerParams(vmem_limit_bytes=16 * 1024 * 1024),
    )(
        hidden,
        norm_gain.reshape(1, features),
        route_expert.reshape(1, tokens),
        priority.reshape(1, tokens),
        route_weight.reshape(1, tokens),
    )


def down_kernel(
    devices, cap_rows, units_ref, down_ref, rows_ref, asked_ref, scale_ref,
    share_ref, weight_ref, many_ref, spread_ref, hidden_ref,
):
    count = units_ref.shape[1] // devices
    chunk = share_ref.shape[0] // devices

    @pl.when(pl.program_id(0) == 0)
    def _():
        for device in range(devices):
            rows = pl.ds(device * count, count)
            gate = units_ref[0, rows, :] * (1.0 / ROW_SCALE)
            up = units_ref[1, rows, :] * (1.0 / ROW_SCALE)
            spread_ref[pl.ds(device * chunk, count), :] = gate * up / (1.0 + jnp.exp(-gate))
        hidden_ref[...] = spread_ref[: devices * chunk, :].astype(jnp.bfloat16)

        slots = LANES // 2
        lane = lax.broadcasted_iota(jnp.int32, (1, LANES), 1)
        asked = asked_ref[...]
        ahead = jnp.zeros((asked.shape[0], LANES), jnp.float32)
        held = []
        for device in range(devices):
            tile = rows_ref[pl.ds(device * count + count - 16, 16), :LANES].astype(jnp.float32)
            code = tile[15:16, :]
            whole = jnp.where(lane < slots, code * RADIX + pltpu.roll(code, slots, 1), 2.0 * NO_TOKEN)
            held.append(whole)
            ahead += (whole < asked).astype(jnp.float32)
        rank = jnp.sum(ahead, axis=1, keepdims=True)
        weight_ref[...] = jnp.where(
            (asked < NO_TOKEN) & (rank < cap_rows), scale_ref[...], 0.0
        )
        table = jnp.concatenate(held, axis=0)
        last = jnp.sum(
            jnp.where(lax.broadcasted_iota(jnp.int32, table.shape, 1) == count - 1, table, 0.0),
            axis=1,
            keepdims=True,
        )
        ahead = jnp.zeros((devices, LANES), jnp.float32)
        for whole in held:
            ahead += (whole < last).astype(jnp.float32)
        rank = jnp.sum(ahead, axis=1, keepdims=True)
        many = jnp.where((last < NO_TOKEN) & (rank < cap_rows), 1.0, 0.0)
        many_ref[0, 0] = jnp.max(many).astype(jnp.int32)

    share_ref[...] = jnp.dot(
        hidden_ref[...], down_ref[...], preferred_element_type=jnp.float32
    ).astype(jnp.bfloat16)


def down_share(units, expert_down, rows, asked, scale, devices, cap_rows):
    _, slots, fr_dev = units.shape
    features = expert_down.shape[1]
    count = slots // devices
    chunks = devices * (count - 1)
    return pl.pallas_call(
        functools.partial(down_kernel, devices, cap_rows),
        grid=(pl.cdiv(features, COLUMNS),),
        in_specs=[
            pl.BlockSpec(memory_space=VMEM),
            pl.BlockSpec((fr_dev, COLUMNS), lambda i: (0, i)),
            pl.BlockSpec((slots, LANES), lambda i: (0, 0)),
            pl.BlockSpec(memory_space=VMEM),
            pl.BlockSpec(memory_space=VMEM),
        ],
        out_specs=(
            pl.BlockSpec((chunks, COLUMNS), lambda i: (0, i)),
            pl.BlockSpec(asked.shape, lambda i: (0, 0)),
            pl.BlockSpec(memory_space=pltpu.SMEM),
        ),
        out_shape=(
            jax.ShapeDtypeStruct((chunks, features), jnp.bfloat16),
            jax.ShapeDtypeStruct(asked.shape, jnp.float32),
            jax.ShapeDtypeStruct((1, 1), jnp.int32),
        ),
        scratch_shapes=[
            VMEM((slots, fr_dev), jnp.float32),
            VMEM((chunks, fr_dev), jnp.bfloat16),
        ],
        compiler_params=pltpu.CompilerParams(vmem_limit_bytes=28 * 1024 * 1024),
        cost_estimate=pl.CostEstimate(
            flops=2 * chunks * fr_dev * features,
            bytes_accessed=2 * fr_dev * features + 2 * chunks * features,
            transcendentals=slots * fr_dev,
        ),
    )(units, expert_down, rows, asked, scale)


def expert_units(rows, expert_gate_up):
    return jnp.einsum("td,dgf->gtf", rows, expert_gate_up, preferred_element_type=jnp.float32)


def wide_share(rows, expert_gate_up, expert_down, chunk):
    devices, count, features = rows.shape
    fr_dev = expert_down.shape[0]
    normed = rows.reshape(devices * count, features).astype(jnp.bfloat16)
    units = expert_units(normed, expert_gate_up) * (1.0 / ROW_SCALE)
    hidden = (jax.nn.silu(units[0]) * units[1]).astype(jnp.bfloat16)
    hidden = jnp.pad(
        hidden.reshape(devices, count, fr_dev), ((0, 0), (0, chunk - count), (0, 0))
    )
    return jnp.dot(
        hidden.reshape(devices * chunk, fr_dev), expert_down, preferred_element_type=jnp.float32
    ).astype(jnp.bfloat16)


def on_device(hidden, norm_gain, route_expert, route_weight, priority, expert_gate_up, expert_down):
    devices = lax.axis_size("sx")
    tok_dev = hidden.shape[0]
    slot_count = tok_dev // 2
    cap_rows = 3 * slot_count * devices // 8
    first, every, slot, asked, scale = pack(
        hidden, norm_gain, route_expert, priority, route_weight
    )
    gathered = lax.all_gather(first.astype(jnp.float16), "sx", axis=0, tiled=True)
    rows = lax.optimization_barrier(gathered.astype(jnp.bfloat16))
    units = expert_units(rows, expert_gate_up)
    share, weight, many = down_share(
        units, expert_down, rows, asked, scale, devices, cap_rows
    )

    def finish(returned):
        place = (
            jnp.arange(returned.shape[0], dtype=jnp.int32)[None, :] == slot.reshape(tok_dev, 1)
        ).astype(jnp.bfloat16)
        routed = jnp.dot(place, returned, preferred_element_type=jnp.float32)
        return (hidden.astype(jnp.float32) + weight * routed).astype(jnp.bfloat16)

    def narrow(share, every):
        return finish(lax.psum_scatter(share, "sx", scatter_dimension=0, tiled=True))

    def wide(share, every):
        rows = lax.all_gather(every.astype(jnp.float16), "sx", axis=0, tiled=False)
        share = wide_share(rows, expert_gate_up, expert_down, slot_count + 15)
        return finish(lax.psum_scatter(share, "sx", scatter_dimension=0, tiled=True))

    return lax.cond(many[0, 0] > 0, wide, narrow, share, every)


def solution(mesh):
    in_specs = (
        P(("dp", "sx"), None),
        P(),
        P(("dp", "sx"), None),
        P(("dp", "sx")),
        P(("dp", "sx")),
        P(None, None, "sx"),
        P("sx", None),
    )
    out_specs = P(("dp", "sx"), None)
    return jax.shard_map(
        on_device, mesh=mesh, in_specs=in_specs, out_specs=out_specs, check_vma=False
    )
```

```python
import functools

import jax
import jax.numpy as jnp
from jax import lax
from jax.experimental import pallas as pl
from jax.experimental.pallas import tpu as pltpu
from jax.sharding import PartitionSpec as P

ROW_SCALE = 256.0
NO_TOKEN = 4096
RADIX = 64
LANES = 128
ROW_BLOCK = 256
VMEM = pltpu.VMEM


def as_column(row):
    n = row.shape[1]
    square = lax.broadcasted_iota(jnp.int32, (n, n), 0) == lax.broadcasted_iota(
        jnp.int32, (n, n), 1
    )
    return jnp.sum(jnp.where(square, row, jnp.zeros_like(row)), axis=1, keepdims=True)


def pack_kernel(
    hidden_hbm, gain_hbm, own_hbm, first_ref, all_ref, slot_ref, asked_ref,
    hidden_ref, gain_ref, own_ref, arrived,
):
    copies = [
        pltpu.make_async_copy(source, target, arrived.at[i])
        for i, (source, target) in enumerate(
            (
                (own_hbm, own_ref),
                (gain_hbm, gain_ref),
                (hidden_hbm, hidden_ref),
            )
        )
    ]
    for copy in copies:
        copy.start()
    for copy in copies[:2]:
        copy.wait()
    slots, features = all_ref.shape
    few = first_ref.shape[0]
    tokens = hidden_ref.shape[0]
    own = own_ref[...]
    own_column = as_column(own)
    slot_row = jnp.sum((own_column < own).astype(jnp.float32), axis=0, keepdims=True)
    slot_column = jnp.sum((own < own_column).astype(jnp.float32), axis=1, keepdims=True)
    slot_row = jnp.where(own < NO_TOKEN, slot_row, float(slots))
    slot_column = jnp.where(own_column < NO_TOKEN, slot_column, float(slots))
    slot_ref[...] = slot_row.astype(jnp.int32)
    asked_ref[...] = own_column
    place = lax.broadcasted_iota(jnp.int32, (slots, tokens), 0).astype(jnp.float32) == slot_row
    selector = jnp.where(place, ROW_SCALE, 0.0).astype(jnp.bfloat16)

    lane = lax.broadcasted_iota(jnp.int32, (tokens, LANES), 1)
    holds = lax.rem(lane, slots).astype(jnp.float32) == slot_column
    held = NO_TOKEN + jnp.sum(
        jnp.where(holds, own_column - NO_TOKEN, 0.0), axis=0, keepdims=True
    )
    quotient = jnp.floor(held * (1.0 / RADIX))
    low = lax.broadcasted_iota(jnp.int32, (1, LANES), 1) < slots
    code = jnp.where(low, quotient, held - quotient * RADIX)

    gain = gain_ref[...].astype(jnp.float32)
    copies[2].wait()
    resid = hidden_ref[...].astype(jnp.float32)
    scale = lax.rsqrt(jnp.mean(resid * resid, axis=1, keepdims=True) + 1e-06)
    for block in range(features // LANES):
        lanes = slice(block * LANES, (block + 1) * LANES)
        hidden_ref[:, lanes] = (
            hidden_ref[:, lanes].astype(jnp.float32) * scale * gain[block : block + 1, :]
        ).astype(jnp.bfloat16)
    packed = jnp.dot(selector, hidden_ref[...], preferred_element_type=jnp.float32)
    all_ref[...] = packed.astype(jnp.bfloat16)
    row = lax.broadcasted_iota(jnp.int32, (few, LANES), 0)
    first_ref[:, LANES:] = packed[:few, LANES:].astype(jnp.bfloat16)
    first_ref[:, :LANES] = jnp.where(row == few - 1, code, packed[:few, :LANES]).astype(
        jnp.bfloat16
    )


def pack(hidden, norm_gain, own):
    tokens, features = hidden.shape
    slots = tokens // 2
    few = 3 * slots // 4
    return pl.pallas_call(
        pack_kernel,
        in_specs=[pl.BlockSpec(memory_space=pltpu.HBM)] * 3,
        out_shape=(
            jax.ShapeDtypeStruct((few, features), jnp.bfloat16),
            jax.ShapeDtypeStruct((slots, features), jnp.bfloat16),
            jax.ShapeDtypeStruct((1, tokens), jnp.int32),
            jax.ShapeDtypeStruct((tokens, 1), jnp.float32),
        ),
        scratch_shapes=[
            VMEM((tokens, features), jnp.bfloat16),
            VMEM((features // LANES, LANES), jnp.bfloat16),
            VMEM((1, tokens), jnp.float32),
            pltpu.SemaphoreType.DMA((3,)),
        ],
        compiler_params=pltpu.CompilerParams(vmem_limit_bytes=16 * 1024 * 1024),
    )(hidden, norm_gain.reshape(features // LANES, LANES), own.reshape(1, tokens))


def rank_kernel(devices, cap_rows, rows_ref, asked_ref, scale_ref, weight_ref, many_ref):
    count = rows_ref.shape[0] // devices
    slots = LANES // 2
    lane = lax.broadcasted_iota(jnp.int32, (1, LANES), 1)
    asked = asked_ref[...]
    ahead = jnp.zeros((asked.shape[0], LANES), jnp.float32)
    held = []
    for device in range(devices):
        tile = rows_ref[pl.ds(device * count + count - 16, 16), :LANES].astype(jnp.float32)
        code = tile[15:16, :]
        whole = jnp.where(lane < slots, code * RADIX + pltpu.roll(code, slots, 1), 2.0 * NO_TOKEN)
        held.append(whole)
        ahead += (whole < asked).astype(jnp.float32)
    rank = jnp.sum(ahead, axis=1, keepdims=True)
    weight_ref[...] = jnp.where((asked < NO_TOKEN) & (rank < cap_rows), as_column(scale_ref[...]), 0.0)
    table = jnp.concatenate(held, axis=0)
    last = jnp.sum(
        jnp.where(lax.broadcasted_iota(jnp.int32, table.shape, 1) == count - 1, table, 0.0),
        axis=1,
        keepdims=True,
    )
    ahead = jnp.zeros((devices, LANES), jnp.float32)
    for whole in held:
        ahead += (whole < last).astype(jnp.float32)
    rank = jnp.sum(ahead, axis=1, keepdims=True)
    many = jnp.where((last < NO_TOKEN) & (rank < cap_rows), 1.0, 0.0)
    many_ref[0, 0] = jnp.max(many).astype(jnp.int32)


def ranks(rows, asked, scale, devices, cap_rows):
    return pl.pallas_call(
        functools.partial(rank_kernel, devices, cap_rows),
        in_specs=[pl.BlockSpec(memory_space=VMEM)] * 3,
        out_specs=(
            pl.BlockSpec(memory_space=VMEM),
            pl.BlockSpec(memory_space=pltpu.SMEM),
        ),
        out_shape=(
            jax.ShapeDtypeStruct(asked.shape, jnp.float32),
            jax.ShapeDtypeStruct((1, 1), jnp.int32),
        ),
        compiler_params=pltpu.CompilerParams(vmem_limit_bytes=8 * 1024 * 1024),
    )(rows, asked, scale)


def down_kernel(devices, units_ref, down_ref, share_hbm, spread_ref, hidden_ref, share_ref, sent):
    count = units_ref.shape[1] // devices
    rows = share_ref.shape[0]
    chunk = rows // devices
    copies = []
    ready = 0
    for block, start in enumerate(range(0, rows, ROW_BLOCK)):
        stop = min(rows, start + ROW_BLOCK)
        while ready < devices and ready * chunk < stop:
            slots = pl.ds(ready * count, count)
            gate = units_ref[0, slots, :] * (1.0 / ROW_SCALE)
            up = units_ref[1, slots, :] * (1.0 / ROW_SCALE)
            spread_ref[pl.ds(ready * chunk, count), :] = gate * up / (1.0 + jnp.exp(-gate))
            ready += 1
        hidden_ref[start:stop, :] = spread_ref[start:stop, :].astype(jnp.bfloat16)
        share_ref[start:stop, :] = jnp.dot(
            hidden_ref[start:stop, :], down_ref[...], preferred_element_type=jnp.float32
        ).astype(jnp.bfloat16)
        copy = pltpu.make_async_copy(
            share_ref.at[start:stop, :], share_hbm.at[start:stop, :], sent.at[block]
        )
        copy.start()
        copies.append(copy)
    for copy in copies:
        copy.wait()


def down_share(units, expert_down, devices):
    _, slots, fr_dev = units.shape
    features = expert_down.shape[1]
    chunks = slots - devices
    return pl.pallas_call(
        functools.partial(down_kernel, devices),
        in_specs=[pl.BlockSpec(memory_space=VMEM)] * 2,
        out_specs=pl.BlockSpec(memory_space=pltpu.HBM),
        out_shape=jax.ShapeDtypeStruct((chunks, features), jnp.bfloat16),
        scratch_shapes=[
            VMEM((slots, fr_dev), jnp.float32),
            VMEM((chunks, fr_dev), jnp.bfloat16),
            VMEM((chunks, features), jnp.bfloat16),
            pltpu.SemaphoreType.DMA((pl.cdiv(chunks, ROW_BLOCK),)),
        ],
        compiler_params=pltpu.CompilerParams(vmem_limit_bytes=24 * 1024 * 1024),
        cost_estimate=pl.CostEstimate(
            flops=2 * chunks * fr_dev * features,
            bytes_accessed=2 * fr_dev * features + 2 * chunks * features,
            transcendentals=slots * fr_dev,
        ),
    )(units, expert_down)


def expert_units(rows, expert_gate_up):
    return jnp.einsum("td,dgf->gtf", rows, expert_gate_up, preferred_element_type=jnp.float32)


def wide_share(rows, expert_gate_up, expert_down, chunk):
    devices, count, features = rows.shape
    fr_dev = expert_down.shape[0]
    normed = rows.reshape(devices * count, features).astype(jnp.bfloat16)
    units = expert_units(normed, expert_gate_up) * (1.0 / ROW_SCALE)
    hidden = (jax.nn.silu(units[0]) * units[1]).astype(jnp.bfloat16)
    hidden = jnp.pad(
        hidden.reshape(devices, count, fr_dev), ((0, 0), (0, chunk - count), (0, 0))
    )
    return jnp.dot(
        hidden.reshape(devices * chunk, fr_dev), expert_down, preferred_element_type=jnp.float32
    ).astype(jnp.bfloat16)


def on_device(hidden, norm_gain, route_expert, route_weight, priority, expert_gate_up, expert_down):
    devices = lax.axis_size("sx")
    tok_dev = hidden.shape[0]
    slot_count = tok_dev // 2
    cap_rows = 3 * slot_count * devices // 8
    own = jnp.where(route_expert[:, 0] == 0, priority, NO_TOKEN).astype(jnp.float32)
    first, every, slot, asked = pack(hidden, norm_gain, own)
    gathered = lax.all_gather(first.astype(jnp.float16), "sx", axis=0, tiled=True)
    rows = lax.optimization_barrier(gathered.astype(jnp.bfloat16))
    weight, many = ranks(rows, asked, route_weight.reshape(1, tok_dev), devices, cap_rows)
    rows, weight, crowded = lax.optimization_barrier((rows, weight, many[0, 0] > 0))
    share = down_share(expert_units(rows, expert_gate_up), expert_down, devices)

    def finish(returned):
        place = (
            jnp.arange(returned.shape[0], dtype=jnp.int32)[None, :] == slot.reshape(tok_dev, 1)
        ).astype(jnp.bfloat16)
        routed = jnp.dot(place, returned, preferred_element_type=jnp.float32)
        return (hidden.astype(jnp.float32) + weight * routed).astype(jnp.bfloat16)

    def narrow(share, every):
        return finish(lax.psum_scatter(share, "sx", scatter_dimension=0, tiled=True))

    def wide(share, every):
        rows = lax.all_gather(every.astype(jnp.float16), "sx", axis=0, tiled=False)
        share = wide_share(rows, expert_gate_up, expert_down, slot_count + 15)
        return finish(lax.psum_scatter(share, "sx", scatter_dimension=0, tiled=True))

    return lax.cond(crowded, wide, narrow, share, every)


def solution(mesh):
    in_specs = (
        P(("dp", "sx"), None),
        P(),
        P(("dp", "sx"), None),
        P(("dp", "sx")),
        P(("dp", "sx")),
        P(None, None, "sx"),
        P("sx", None),
    )
    out_specs = P(("dp", "sx"), None)
    return jax.shard_map(
        on_device, mesh=mesh, in_specs=in_specs, out_specs=out_specs, check_vma=False
    )
```

```python
import functools

import jax
import jax.numpy as jnp
from jax import lax
from jax.experimental import pallas as pl
from jax.experimental.pallas import tpu as pltpu
from jax.sharding import PartitionSpec as P

ROW_SCALE = 256.0
NO_TOKEN = 4096
RADIX = 64
LANES = 128
COLUMNS = 640
SPARE = 16
BLOCKS = (6, 6, 4)
VMEM = pltpu.VMEM


def as_column(row):
    n = row.shape[1]
    square = lax.broadcasted_iota(jnp.int32, (n, n), 0) == lax.broadcasted_iota(
        jnp.int32, (n, n), 1
    )
    return jnp.sum(jnp.where(square, row, jnp.zeros_like(row)), axis=1, keepdims=True)


def pack_kernel(
    hidden_hbm, gain_hbm, own_hbm, first_ref, all_ref, slot_ref, asked_ref,
    hidden_ref, gain_ref, own_ref, arrived,
):
    copies = [
        pltpu.make_async_copy(source, target, arrived.at[i])
        for i, (source, target) in enumerate(
            (
                (own_hbm, own_ref),
                (gain_hbm, gain_ref),
                (hidden_hbm, hidden_ref),
            )
        )
    ]
    for copy in copies:
        copy.start()
    for copy in copies[:2]:
        copy.wait()
    slots, features = all_ref.shape
    few = first_ref.shape[0]
    tokens = hidden_ref.shape[0]
    own = own_ref[...]
    own_column = as_column(own)
    slot_row = jnp.sum((own_column < own).astype(jnp.float32), axis=0, keepdims=True)
    slot_column = jnp.sum((own < own_column).astype(jnp.float32), axis=1, keepdims=True)
    slot_row = jnp.where(own < NO_TOKEN, slot_row, float(slots))
    slot_column = jnp.where(own_column < NO_TOKEN, slot_column, float(slots))
    slot_ref[...] = slot_column.astype(jnp.int32)
    asked_ref[...] = own_column
    place = lax.broadcasted_iota(jnp.int32, (slots, tokens), 0).astype(jnp.float32) == slot_row
    selector = jnp.where(place, ROW_SCALE, 0.0).astype(jnp.bfloat16)

    lane = lax.broadcasted_iota(jnp.int32, (tokens, LANES), 1)
    holds = lax.rem(lane, slots).astype(jnp.float32) == slot_column
    held = NO_TOKEN + jnp.sum(
        jnp.where(holds, own_column - NO_TOKEN, 0.0), axis=0, keepdims=True
    )
    quotient = jnp.floor(held * (1.0 / RADIX))
    low = lax.broadcasted_iota(jnp.int32, (1, LANES), 1) < slots
    code = jnp.where(low, quotient, held - quotient * RADIX)

    gain = gain_ref[...].astype(jnp.float32)
    copies[2].wait()
    resid = hidden_ref[...].astype(jnp.float32)
    scale = lax.rsqrt(jnp.mean(resid * resid, axis=1, keepdims=True) + 1e-06)
    for block in range(features // LANES):
        lanes = slice(block * LANES, (block + 1) * LANES)
        hidden_ref[:, lanes] = (
            hidden_ref[:, lanes].astype(jnp.float32) * scale * gain[block : block + 1, :]
        ).astype(jnp.bfloat16)
    packed = jnp.dot(selector, hidden_ref[...], preferred_element_type=jnp.float32)
    all_ref[...] = packed.astype(jnp.bfloat16)
    row = lax.broadcasted_iota(jnp.int32, (few, LANES), 0)
    first_ref[:, LANES:] = packed[:few, LANES:].astype(jnp.bfloat16)
    first_ref[:, :LANES] = jnp.where(row == few - 1, code, packed[:few, :LANES]).astype(
        jnp.bfloat16
    )


def pack(hidden, norm_gain, own):
    tokens, features = hidden.shape
    slots = tokens // 2
    few = 3 * slots // 4
    return pl.pallas_call(
        pack_kernel,
        in_specs=[pl.BlockSpec(memory_space=pltpu.HBM)] * 3,
        out_shape=(
            jax.ShapeDtypeStruct((few, features), jnp.bfloat16),
            jax.ShapeDtypeStruct((slots, features), jnp.bfloat16),
            jax.ShapeDtypeStruct((tokens, 1), jnp.int32),
            jax.ShapeDtypeStruct((tokens, 1), jnp.float32),
        ),
        scratch_shapes=[
            VMEM((tokens, features), jnp.bfloat16),
            VMEM((features // LANES, LANES), jnp.bfloat16),
            VMEM((1, tokens), jnp.float32),
            pltpu.SemaphoreType.DMA((3,)),
        ],
        compiler_params=pltpu.CompilerParams(vmem_limit_bytes=16 * 1024 * 1024),
    )(hidden, norm_gain.reshape(features // LANES, LANES), own.reshape(1, tokens))


def rank_kernel(devices, cap_rows, rows_ref, asked_ref, scale_ref, weight_ref, many_ref):
    count = rows_ref.shape[0] // devices
    slots = LANES // 2
    lane = lax.broadcasted_iota(jnp.int32, (1, LANES), 1)
    asked = asked_ref[...]
    ahead = jnp.zeros((asked.shape[0], LANES), jnp.float32)
    held = []
    for device in range(devices):
        tile = rows_ref[pl.ds(device * count + count - 16, 16), :LANES].astype(jnp.float32)
        code = tile[15:16, :]
        whole = jnp.where(lane < slots, code * RADIX + pltpu.roll(code, slots, 1), 2.0 * NO_TOKEN)
        held.append(whole)
        ahead += (whole < asked).astype(jnp.float32)
    rank = jnp.sum(ahead, axis=1, keepdims=True)
    weight_ref[...] = jnp.where((asked < NO_TOKEN) & (rank < cap_rows), as_column(scale_ref[...]), 0.0)
    table = jnp.concatenate(held, axis=0)
    last = jnp.sum(
        jnp.where(lax.broadcasted_iota(jnp.int32, table.shape, 1) == count - 1, table, 0.0),
        axis=1,
        keepdims=True,
    )
    ahead = jnp.zeros((devices, LANES), jnp.float32)
    for whole in held:
        ahead += (whole < last).astype(jnp.float32)
    rank = jnp.sum(ahead, axis=1, keepdims=True)
    many = jnp.where((last < NO_TOKEN) & (rank < cap_rows), 1.0, 0.0)
    many_ref[0, 0] = jnp.max(many).astype(jnp.int32)


def ranks(rows, asked, scale, devices, cap_rows):
    return pl.pallas_call(
        functools.partial(rank_kernel, devices, cap_rows),
        in_specs=[pl.BlockSpec(memory_space=VMEM)] * 3,
        out_specs=(
            pl.BlockSpec(memory_space=VMEM),
            pl.BlockSpec(memory_space=pltpu.SMEM),
        ),
        out_shape=(
            jax.ShapeDtypeStruct(asked.shape, jnp.float32),
            jax.ShapeDtypeStruct((1, 1), jnp.int32),
        ),
        compiler_params=pltpu.CompilerParams(vmem_limit_bytes=8 * 1024 * 1024),
    )(rows, asked, scale)


def down_kernel(part, units_ref, down_ref, share_hbm, hidden_ref, share_ref, sent):
    fr_dev, features = down_ref.shape
    devices = sum(BLOCKS)
    count = units_ref.shape[1] // devices
    rows = share_ref.shape[0]
    copies = []
    first = 0
    for block, held in enumerate(BLOCKS):
        slots = slice(first * count, (first + held) * count)
        gate = units_ref[0, slots, :] * (1.0 / ROW_SCALE)
        up = units_ref[1, slots, :] * (1.0 / ROW_SCALE)
        hidden_ref[slots, :] = (gate * up / (1.0 + jnp.exp(-gate))).astype(jnp.bfloat16)
        sums = jnp.dot(hidden_ref[slots, :], down_ref[...], preferred_element_type=jnp.float32)
        for device in range(held):
            start = (first + device) * part
            for column in range(features // COLUMNS):
                share_ref[start : start + count, :] = sums[
                    device * count : (device + 1) * count,
                    column * COLUMNS : (column + 1) * COLUMNS,
                ].astype(jnp.bfloat16)
                start += count
            stop = min((first + device + 1) * part, rows)
            if start < stop:
                share_ref[start:stop, :] = jnp.zeros((stop - start, COLUMNS), jnp.bfloat16)
        span = slice(first * part, min((first + held) * part, rows))
        copy = pltpu.make_async_copy(share_ref.at[span, :], share_hbm.at[span, :], sent.at[block])
        copy.start()
        copies.append(copy)
        first += held
    for copy in copies:
        copy.wait()


def down_share(units, expert_down, devices):
    _, slots, fr_dev = units.shape
    features = expert_down.shape[1]
    part = features // COLUMNS * (slots // devices) + SPARE
    rows = devices * (part - 1)
    return pl.pallas_call(
        functools.partial(down_kernel, part),
        in_specs=[pl.BlockSpec(memory_space=VMEM)] * 2,
        out_specs=pl.BlockSpec(memory_space=pltpu.HBM),
        out_shape=jax.ShapeDtypeStruct((rows, COLUMNS), jnp.bfloat16),
        scratch_shapes=[
            VMEM((slots, fr_dev), jnp.bfloat16),
            VMEM((rows, COLUMNS), jnp.bfloat16),
            pltpu.SemaphoreType.DMA((len(BLOCKS),)),
        ],
        compiler_params=pltpu.CompilerParams(vmem_limit_bytes=28 * 1024 * 1024),
        cost_estimate=pl.CostEstimate(
            flops=2 * slots * fr_dev * features,
            bytes_accessed=2 * fr_dev * features + 2 * rows * COLUMNS,
            transcendentals=slots * fr_dev,
        ),
    )(units, expert_down)


def expert_units(rows, expert_gate_up):
    return jnp.einsum("td,dgf->gtf", rows, expert_gate_up, preferred_element_type=jnp.float32)


def finish_kernel(
    chunk_ref, slot_ref, weight_ref, hidden_ref, out_hbm, out_ref, sent
):
    tokens, features = hidden_ref.shape
    rows = chunk_ref.shape[0]
    columns = features // COLUMNS
    count = (rows + 1 - SPARE) // columns
    row = lax.broadcasted_iota(jnp.int32, (tokens, rows), 1) - lax.axis_index("sx")
    copies = []
    for column in range(columns):
        lanes = slice(column * COLUMNS, (column + 1) * COLUMNS)
        place = jnp.where(row == slot_ref[...] + column * count, 1.0, 0.0).astype(jnp.bfloat16)
        routed = jnp.dot(place, chunk_ref[...], preferred_element_type=jnp.float32)
        out_ref[:, lanes] = (
            hidden_ref[:, lanes].astype(jnp.float32) + weight_ref[...] * routed
        ).astype(jnp.bfloat16)
        copy = pltpu.make_async_copy(out_ref.at[:, lanes], out_hbm.at[:, lanes], sent.at[column])
        copy.start()
        copies.append(copy)
    for copy in copies:
        copy.wait()


def finish(chunk, slot, weight, hidden):
    return pl.pallas_call(
        finish_kernel,
        in_specs=[pl.BlockSpec(memory_space=VMEM)] * 4,
        out_specs=pl.BlockSpec(memory_space=pltpu.HBM),
        out_shape=jax.ShapeDtypeStruct(hidden.shape, hidden.dtype),
        scratch_shapes=[
            VMEM(hidden.shape, hidden.dtype),
            pltpu.SemaphoreType.DMA((hidden.shape[1] // COLUMNS,)),
        ],
        compiler_params=pltpu.CompilerParams(vmem_limit_bytes=8 * 1024 * 1024),
    )(chunk, slot, weight, hidden)


def wide_share(rows, expert_gate_up, expert_down, chunk):
    devices, count, features = rows.shape
    fr_dev = expert_down.shape[0]
    normed = rows.reshape(devices * count, features).astype(jnp.bfloat16)
    units = expert_units(normed, expert_gate_up) * (1.0 / ROW_SCALE)
    hidden = (jax.nn.silu(units[0]) * units[1]).astype(jnp.bfloat16)
    hidden = jnp.pad(
        hidden.reshape(devices, count, fr_dev), ((0, 0), (0, chunk - count), (0, 0))
    )
    return jnp.dot(
        hidden.reshape(devices * chunk, fr_dev), expert_down, preferred_element_type=jnp.float32
    ).astype(jnp.bfloat16)


def on_device(hidden, norm_gain, route_expert, route_weight, priority, expert_gate_up, expert_down):
    devices = lax.axis_size("sx")
    tok_dev = hidden.shape[0]
    slot_count = tok_dev // 2
    cap_rows = 3 * slot_count * devices // 8
    own = jnp.where(route_expert[:, 0] == 0, priority, NO_TOKEN).astype(jnp.float32)
    first, every, slot, asked = pack(hidden, norm_gain, own)
    gathered = lax.all_gather(first.astype(jnp.float16), "sx", axis=0, tiled=True)
    rows = lax.optimization_barrier(gathered.astype(jnp.bfloat16))
    weight, many = ranks(rows, asked, route_weight.reshape(1, tok_dev), devices, cap_rows)
    rows, weight, crowded = lax.optimization_barrier((rows, weight, many[0, 0] > 0))
    share = down_share(expert_units(rows, expert_gate_up), expert_down, devices)

    def narrow(share, every):
        chunk = lax.psum_scatter(share, "sx", scatter_dimension=0, tiled=True)
        return finish(chunk, slot, weight, hidden)

    def wide(share, every):
        rows = lax.all_gather(every.astype(jnp.float16), "sx", axis=0, tiled=False)
        share = wide_share(rows, expert_gate_up, expert_down, slot_count + 15)
        returned = lax.psum_scatter(share, "sx", scatter_dimension=0, tiled=True)
        place = (jnp.arange(slot_count + 15, dtype=jnp.int32)[None, :] == slot).astype(jnp.bfloat16)
        routed = jnp.dot(place, returned, preferred_element_type=jnp.float32)
        return (hidden.astype(jnp.float32) + weight * routed).astype(jnp.bfloat16)

    return lax.cond(crowded, wide, narrow, share, every)


def solution(mesh):
    in_specs = (
        P(("dp", "sx"), None),
        P(),
        P(("dp", "sx"), None),
        P(("dp", "sx")),
        P(("dp", "sx")),
        P(None, None, "sx"),
        P("sx", None),
    )
    out_specs = P(("dp", "sx"), None)
    return jax.shard_map(
        on_device, mesh=mesh, in_specs=in_specs, out_specs=out_specs, check_vma=False
    )
```

```python
import functools

import jax
import jax.numpy as jnp
from jax import lax
from jax.experimental import pallas as pl
from jax.experimental.pallas import tpu as pltpu
from jax.sharding import PartitionSpec as P

ROW_SCALE = 256.0
NO_TOKEN = 4096
RADIX = 64
LANES = 128
TILE = 16
FEW = 40
COLUMNS = 640
SPARE = TILE
BLOCKS = (6, 6, 4)
FEW_BLOCKS = (6, 6, 4)
VMEM = pltpu.VMEM


def as_column(row):
    n = row.shape[1]
    square = lax.broadcasted_iota(jnp.int32, (n, n), 0) == lax.broadcasted_iota(
        jnp.int32, (n, n), 1
    )
    return jnp.sum(jnp.where(square, row, jnp.zeros_like(row)), axis=1, keepdims=True)


def pack_kernel(
    hidden_hbm, gain_hbm, own_hbm, first_ref, all_ref, slot_ref, asked_ref,
    hidden_ref, gain_ref, own_ref, arrived,
):
    copies = [
        pltpu.make_async_copy(source, target, arrived.at[i])
        for i, (source, target) in enumerate(
            (
                (own_hbm, own_ref),
                (gain_hbm, gain_ref),
                (hidden_hbm, hidden_ref),
            )
        )
    ]
    for copy in copies:
        copy.start()
    for copy in copies[:2]:
        copy.wait()
    slots, features = all_ref.shape
    few = first_ref.shape[0]
    tokens = hidden_ref.shape[0]
    own = own_ref[...]
    own_column = as_column(own)
    slot_row = jnp.sum((own_column < own).astype(jnp.float32), axis=0, keepdims=True)
    slot_column = jnp.sum((own < own_column).astype(jnp.float32), axis=1, keepdims=True)
    slot_row = jnp.where(own < NO_TOKEN, slot_row, float(slots))
    slot_column = jnp.where(own_column < NO_TOKEN, slot_column, float(slots))
    slot_ref[...] = slot_column.astype(jnp.int32)
    asked_ref[...] = own_column
    place = lax.broadcasted_iota(jnp.int32, (slots, tokens), 0).astype(jnp.float32) == slot_row
    selector = jnp.where(place, ROW_SCALE, 0.0).astype(jnp.bfloat16)

    lane = lax.broadcasted_iota(jnp.int32, (tokens, LANES), 1)
    holds = lax.rem(lane, slots).astype(jnp.float32) == slot_column
    held = NO_TOKEN + jnp.sum(
        jnp.where(holds, own_column - NO_TOKEN, 0.0), axis=0, keepdims=True
    )
    quotient = jnp.floor(held * (1.0 / RADIX))
    low = lax.broadcasted_iota(jnp.int32, (1, LANES), 1) < slots
    code = jnp.where(low, quotient, held - quotient * RADIX)

    gain = gain_ref[...].astype(jnp.float32)
    copies[2].wait()
    resid = hidden_ref[...].astype(jnp.float32)
    scale = lax.rsqrt(jnp.mean(resid * resid, axis=1, keepdims=True) + 1e-06)
    for block in range(features // LANES):
        lanes = slice(block * LANES, (block + 1) * LANES)
        hidden_ref[:, lanes] = (
            hidden_ref[:, lanes].astype(jnp.float32) * scale * gain[block : block + 1, :]
        ).astype(jnp.bfloat16)
    packed = jnp.dot(selector, hidden_ref[...], preferred_element_type=jnp.float32)
    all_ref[...] = packed.astype(jnp.bfloat16)
    row = lax.broadcasted_iota(jnp.int32, (few, LANES), 0)
    first_ref[:, LANES:] = packed[:few, LANES:].astype(jnp.bfloat16)
    first_ref[:, :LANES] = jnp.where(row == few - 1, code, packed[:few, :LANES]).astype(
        jnp.bfloat16
    )


def pack(hidden, norm_gain, own):
    tokens, features = hidden.shape
    slots = tokens // 2
    few = 3 * slots // 4
    return pl.pallas_call(
        pack_kernel,
        in_specs=[pl.BlockSpec(memory_space=pltpu.HBM)] * 3,
        out_shape=(
            jax.ShapeDtypeStruct((few, features), jnp.bfloat16),
            jax.ShapeDtypeStruct((slots, features), jnp.bfloat16),
            jax.ShapeDtypeStruct((tokens, 1), jnp.int32),
            jax.ShapeDtypeStruct((tokens, 1), jnp.float32),
        ),
        scratch_shapes=[
            VMEM((tokens, features), jnp.bfloat16),
            VMEM((features // LANES, LANES), jnp.bfloat16),
            VMEM((1, tokens), jnp.float32),
            pltpu.SemaphoreType.DMA((3,)),
        ],
        compiler_params=pltpu.CompilerParams(vmem_limit_bytes=16 * 1024 * 1024),
    )(hidden, norm_gain.reshape(features // LANES, LANES), own.reshape(1, tokens))


def rank_kernel(devices, cap_rows, rows_ref, asked_ref, scale_ref, weight_ref, level_ref):
    count = rows_ref.shape[0] // devices
    slots = LANES // 2
    lane = lax.broadcasted_iota(jnp.int32, (1, LANES), 1)
    asked = asked_ref[...]
    ahead = jnp.zeros((asked.shape[0], LANES), jnp.float32)
    held = []
    for device in range(devices):
        tile = rows_ref[pl.ds(device * count + count - 16, 16), :LANES].astype(jnp.float32)
        code = tile[15:16, :]
        whole = jnp.where(lane < slots, code * RADIX + pltpu.roll(code, slots, 1), 2.0 * NO_TOKEN)
        held.append(whole)
        ahead += (whole < asked).astype(jnp.float32)
    rank = jnp.sum(ahead, axis=1, keepdims=True)
    weight_ref[...] = jnp.where((asked < NO_TOKEN) & (rank < cap_rows), as_column(scale_ref[...]), 0.0)
    table = jnp.concatenate(held, axis=0)
    column = lax.broadcasted_iota(jnp.int32, table.shape, 1)
    level = jnp.zeros((devices, 1), jnp.float32)
    for edge in (FEW, count - 1):
        asked = jnp.sum(jnp.where(column == edge, table, 0.0), axis=1, keepdims=True)
        ahead = jnp.zeros((devices, LANES), jnp.float32)
        for whole in held:
            ahead += (whole < asked).astype(jnp.float32)
        rank = jnp.sum(ahead, axis=1, keepdims=True)
        level += jnp.where((asked < NO_TOKEN) & (rank < cap_rows), 1.0, 0.0)
    level_ref[0, 0] = jnp.max(level).astype(jnp.int32)


def ranks(rows, asked, scale, devices, cap_rows):
    return pl.pallas_call(
        functools.partial(rank_kernel, devices, cap_rows),
        in_specs=[pl.BlockSpec(memory_space=VMEM)] * 3,
        out_specs=(
            pl.BlockSpec(memory_space=VMEM),
            pl.BlockSpec(memory_space=pltpu.SMEM),
        ),
        out_shape=(
            jax.ShapeDtypeStruct(asked.shape, jnp.float32),
            jax.ShapeDtypeStruct((1, 1), jnp.int32),
        ),
        compiler_params=pltpu.CompilerParams(vmem_limit_bytes=8 * 1024 * 1024),
    )(rows, asked, scale)


def parts(count, features):
    blocks = features // LANES
    whole = FEW // TILE * TILE
    shared = pl.cdiv(blocks * (FEW - whole), TILE) * TILE
    return blocks * count + SPARE, blocks * whole + shared + SPARE


def down_kernel(
    units_ref, down_ref, level_ref, many_hbm, few_hbm, hidden_ref, many_ref, few_ref, sent
):
    fr_dev, features = down_ref.shape
    devices = sum(BLOCKS)
    count = units_ref.shape[1] // devices
    many_part, few_part = parts(count, features)
    blocks = features // LANES
    whole = FEW // TILE * TILE
    rest = FEW - whole
    few = level_ref[0, 0] == 0

    def multiply(first, held, kept):
        ready = []
        for device in range(first, first + held):
            slots = slice(device * count, device * count + kept)
            gate = units_ref[0, slots, :] * (1.0 / ROW_SCALE)
            up = units_ref[1, slots, :] * (1.0 / ROW_SCALE)
            ready.append(gate * up / (1.0 + jnp.exp(-gate)))
        span = slice(first * kept, (first + held) * kept)
        hidden_ref[span, :] = jnp.concatenate(ready, axis=0).astype(jnp.bfloat16)
        return jnp.dot(hidden_ref[span, :], down_ref[...], preferred_element_type=jnp.float32)

    def clear(ref, start, stop):
        if start < stop:
            ref[start:stop, :] = jnp.zeros((stop - start, LANES), jnp.bfloat16)

    def copy(source, target, device, part):
        span = slice(device * part, min((device + 1) * part, source.shape[0]))
        return pltpu.make_async_copy(source.at[span, :], target.at[span, :], sent.at[device])

    @pl.when(few)
    def _():
        first = 0
        for held in FEW_BLOCKS:
            sums = multiply(first, held, FEW)
            for local in range(held):
                device = first + local
                start = device * few_part
                sum_rows = sums[local * FEW : (local + 1) * FEW, :]
                for block in range(blocks):
                    lanes = slice(block * LANES, (block + 1) * LANES)
                    few_ref[start : start + whole, :] = sum_rows[:whole, lanes].astype(jnp.bfloat16)
                    start += whole
                for block in range(0, blocks, TILE // rest):
                    pieces = [
                        sum_rows[whole:, b * LANES : (b + 1) * LANES]
                        if b < blocks
                        else jnp.zeros((rest, LANES), jnp.float32)
                        for b in range(block, block + TILE // rest)
                    ]
                    few_ref[start : start + TILE, :] = jnp.concatenate(pieces, axis=0).astype(
                        jnp.bfloat16
                    )
                    start += TILE
                clear(few_ref, start, min((device + 1) * few_part, few_ref.shape[0]))
                copy(few_ref, few_hbm, device, few_part).start()
            first += held
        for device in range(devices):
            copy(few_ref, few_hbm, device, few_part).wait()

    @pl.when(jnp.logical_not(few))
    def _():
        first = 0
        for held in BLOCKS:
            sums = multiply(first, held, count)
            for local in range(held):
                device = first + local
                start = device * many_part
                for block in range(blocks):
                    many_ref[start : start + count, :] = sums[
                        local * count : (local + 1) * count, block * LANES : (block + 1) * LANES
                    ].astype(jnp.bfloat16)
                    start += count
                clear(many_ref, start, min((device + 1) * many_part, many_ref.shape[0]))
                copy(many_ref, many_hbm, device, many_part).start()
            first += held
        for device in range(devices):
            copy(many_ref, many_hbm, device, many_part).wait()


def down_shares(units, expert_down, level, devices):
    _, slots, fr_dev = units.shape
    features = expert_down.shape[1]
    shapes = [
        (devices * (part - 1), LANES) for part in parts(slots // devices, features)
    ]
    return pl.pallas_call(
        down_kernel,
        in_specs=[
            pl.BlockSpec(memory_space=VMEM),
            pl.BlockSpec(memory_space=VMEM),
            pl.BlockSpec(memory_space=pltpu.SMEM),
        ],
        out_specs=[pl.BlockSpec(memory_space=pltpu.HBM)] * 2,
        out_shape=[jax.ShapeDtypeStruct(shape, jnp.bfloat16) for shape in shapes],
        scratch_shapes=[
            VMEM((slots, fr_dev), jnp.bfloat16),
            VMEM(shapes[0], jnp.bfloat16),
            VMEM(shapes[1], jnp.bfloat16),
            pltpu.SemaphoreType.DMA((devices,)),
        ],
        compiler_params=pltpu.CompilerParams(vmem_limit_bytes=32 * 1024 * 1024),
        cost_estimate=pl.CostEstimate(
            flops=2 * slots * fr_dev * features,
            bytes_accessed=2 * fr_dev * features + 2 * shapes[0][0] * LANES,
            transcendentals=slots * fr_dev,
        ),
    )(units, expert_down, level)


def expert_units(rows, expert_gate_up):
    return jnp.einsum("td,dgf->gtf", rows, expert_gate_up, preferred_element_type=jnp.float32)


def finish_kernel(
    count, chunk_ref, slot_ref, weight_ref, hidden_ref, out_hbm, rows_ref, out_ref, sent
):
    tokens, features = hidden_ref.shape
    blocks = features // LANES
    whole = count // TILE * TILE
    rest = count - whole
    span = whole + SPARE
    shift = lax.axis_index("sx")
    slot = slot_ref[...]

    def places(width, first, last, start):
        row = lax.broadcasted_iota(jnp.int32, (tokens, width), 1)
        hit = (row == slot - first + start + shift) & (slot >= first) & (slot < last)
        return jnp.where(hit, 1.0, 0.0).astype(jnp.bfloat16)

    def window(start, width, row, lanes):
        there = min(width, chunk_ref.shape[0] - start) // TILE * TILE
        rows_ref[row : row + there, lanes] = chunk_ref[start : start + there, :]
        if there < width:
            rows_ref[row + there : row + width, lanes] = jnp.zeros((width - there, LANES), jnp.bfloat16)
            left = chunk_ref.shape[0] - start - there
            rows_ref[row + there : row + there + left, lanes] = chunk_ref[
                start + there : start + there + left, :
            ]

    group = TILE // rest if rest else 0
    shared = [places(2 * TILE, whole, count, piece * rest) for piece in range(group)]
    place = jnp.concatenate([places(span, 0, whole, 0)] + shared, axis=1)
    copies = []
    for step in range(features // COLUMNS):
        for block in range(step * COLUMNS // LANES, (step + 1) * COLUMNS // LANES):
            lanes = slice(block * LANES, (block + 1) * LANES)
            window(block * whole, span, 0, lanes)
            for piece in range(group):
                row = span + piece * 2 * TILE
                if piece == block % group:
                    window(blocks * whole + block // group * TILE, 2 * TILE, row, lanes)
                else:
                    rows_ref[row : row + 2 * TILE, lanes] = jnp.zeros((2 * TILE, LANES), jnp.bfloat16)
        lanes = slice(step * COLUMNS, (step + 1) * COLUMNS)
        routed = jnp.dot(place, rows_ref[:, lanes], preferred_element_type=jnp.float32)
        out_ref[:, lanes] = (
            hidden_ref[:, lanes].astype(jnp.float32) + weight_ref[...] * routed
        ).astype(jnp.bfloat16)
        copy = pltpu.make_async_copy(out_ref.at[:, lanes], out_hbm.at[:, lanes], sent.at[step])
        copy.start()
        copies.append(copy)
    for copy in copies:
        copy.wait()


def finish(count, chunk, slot, weight, hidden):
    rest = count % TILE
    rows = count - rest + SPARE + (TILE // rest * 2 * TILE if rest else 0)
    return pl.pallas_call(
        functools.partial(finish_kernel, count),
        in_specs=[pl.BlockSpec(memory_space=VMEM)] * 4,
        out_specs=pl.BlockSpec(memory_space=pltpu.HBM),
        out_shape=jax.ShapeDtypeStruct(hidden.shape, hidden.dtype),
        scratch_shapes=[
            VMEM((rows, hidden.shape[1]), chunk.dtype),
            VMEM(hidden.shape, hidden.dtype),
            pltpu.SemaphoreType.DMA((hidden.shape[1] // COLUMNS,)),
        ],
        compiler_params=pltpu.CompilerParams(vmem_limit_bytes=8 * 1024 * 1024),
    )(chunk, slot, weight, hidden)


def wide_share(rows, expert_gate_up, expert_down, chunk):
    devices, count, features = rows.shape
    fr_dev = expert_down.shape[0]
    normed = rows.reshape(devices * count, features).astype(jnp.bfloat16)
    units = expert_units(normed, expert_gate_up) * (1.0 / ROW_SCALE)
    hidden = (jax.nn.silu(units[0]) * units[1]).astype(jnp.bfloat16)
    hidden = jnp.pad(
        hidden.reshape(devices, count, fr_dev), ((0, 0), (0, chunk - count), (0, 0))
    )
    return jnp.dot(
        hidden.reshape(devices * chunk, fr_dev), expert_down, preferred_element_type=jnp.float32
    ).astype(jnp.bfloat16)


def on_device(hidden, norm_gain, route_expert, route_weight, priority, expert_gate_up, expert_down):
    devices = lax.axis_size("sx")
    tok_dev = hidden.shape[0]
    slot_count = tok_dev // 2
    cap_rows = 3 * slot_count * devices // 8
    own = jnp.where(route_expert[:, 0] == 0, priority, NO_TOKEN).astype(jnp.float32)
    first, every, slot, asked = pack(hidden, norm_gain, own)
    gathered = lax.all_gather(first.astype(jnp.float16), "sx", axis=0, tiled=True)
    rows = lax.optimization_barrier(gathered.astype(jnp.bfloat16))
    weight, level = ranks(rows, asked, route_weight.reshape(1, tok_dev), devices, cap_rows)
    level = level[0, 0]
    index = lax.clamp(jnp.int32(0), level, jnp.int32(2))
    rows, weight, ready = lax.optimization_barrier((rows, weight, index))
    many_share, few_share = down_shares(
        expert_units(rows, expert_gate_up), expert_down, ready.reshape(1, 1), devices
    )

    def few(many_share, few_share, every):
        chunk = lax.psum_scatter(few_share, "sx", scatter_dimension=0, tiled=True)
        return finish(FEW, chunk, slot, weight, hidden)

    def many(many_share, few_share, every):
        chunk = lax.psum_scatter(many_share, "sx", scatter_dimension=0, tiled=True)
        return finish(first.shape[0], chunk, slot, weight, hidden)

    def wide(many_share, few_share, every):
        rows = lax.all_gather(every.astype(jnp.float16), "sx", axis=0, tiled=False)
        share = wide_share(rows, expert_gate_up, expert_down, slot_count + 15)
        returned = lax.psum_scatter(share, "sx", scatter_dimension=0, tiled=True)
        place = (jnp.arange(slot_count + 15, dtype=jnp.int32)[None, :] == slot).astype(jnp.bfloat16)
        routed = jnp.dot(place, returned, preferred_element_type=jnp.float32)
        return (hidden.astype(jnp.float32) + weight * routed).astype(jnp.bfloat16)

    return lax.switch(level, (few, many, wide), many_share, few_share, every)


def solution(mesh):
    in_specs = (
        P(("dp", "sx"), None),
        P(),
        P(("dp", "sx"), None),
        P(("dp", "sx")),
        P(("dp", "sx")),
        P(None, None, "sx"),
        P("sx", None),
    )
    out_specs = P(("dp", "sx"), None)
    return jax.shard_map(
        on_device, mesh=mesh, in_specs=in_specs, out_specs=out_specs, check_vma=False
    )
```

```python
import functools

import jax
import jax.numpy as jnp
from jax import lax
from jax.experimental import pallas as pl
from jax.experimental.pallas import tpu as pltpu
from jax.sharding import PartitionSpec as P

ROW_SCALE = 256.0
NO_TOKEN = 4096
RADIX = 64
LANES = 128
TILE = 16
FEW = 40
COLUMNS = 640
SPARE = TILE
BLOCKS = (6, 6, 4)
FEW_BLOCKS = (6, 6, 4)
VMEM = pltpu.VMEM


def as_column(row):
    n = row.shape[1]
    square = lax.broadcasted_iota(jnp.int32, (n, n), 0) == lax.broadcasted_iota(
        jnp.int32, (n, n), 1
    )
    return jnp.sum(jnp.where(square, row, jnp.zeros_like(row)), axis=1, keepdims=True)


def pack_kernel(
    hidden_hbm, gain_hbm, own_hbm, first_ref, all_ref, slot_ref, asked_ref,
    hidden_ref, gain_ref, own_ref, arrived,
):
    copies = [
        pltpu.make_async_copy(source, target, arrived.at[i])
        for i, (source, target) in enumerate(
            (
                (own_hbm, own_ref),
                (gain_hbm, gain_ref),
                (hidden_hbm, hidden_ref),
            )
        )
    ]
    for copy in copies:
        copy.start()
    for copy in copies[:2]:
        copy.wait()
    slots, features = all_ref.shape
    few = first_ref.shape[0]
    tokens = hidden_ref.shape[0]
    own = own_ref[...]
    own_column = as_column(own)
    slot_row = jnp.sum((own_column < own).astype(jnp.float32), axis=0, keepdims=True)
    slot_column = jnp.sum((own < own_column).astype(jnp.float32), axis=1, keepdims=True)
    slot_row = jnp.where(own < NO_TOKEN, slot_row, float(slots))
    slot_column = jnp.where(own_column < NO_TOKEN, slot_column, float(slots))
    slot_ref[...] = slot_column.astype(jnp.int32)
    asked_ref[...] = own_column
    place = lax.broadcasted_iota(jnp.int32, (slots, tokens), 0).astype(jnp.float32) == slot_row
    selector = jnp.where(place, ROW_SCALE, 0.0).astype(jnp.bfloat16)

    lane = lax.broadcasted_iota(jnp.int32, (tokens, LANES), 1)
    holds = lax.rem(lane, slots).astype(jnp.float32) == slot_column
    held = NO_TOKEN + jnp.sum(
        jnp.where(holds, own_column - NO_TOKEN, 0.0), axis=0, keepdims=True
    )
    quotient = jnp.floor(held * (1.0 / RADIX))
    low = lax.broadcasted_iota(jnp.int32, (1, LANES), 1) < slots
    code = jnp.where(low, quotient, held - quotient * RADIX)

    gain = gain_ref[...].astype(jnp.float32)
    copies[2].wait()
    resid = hidden_ref[...].astype(jnp.float32)
    scale = lax.rsqrt(jnp.mean(resid * resid, axis=1, keepdims=True) + 1e-06)
    for block in range(features // LANES):
        lanes = slice(block * LANES, (block + 1) * LANES)
        hidden_ref[:, lanes] = (
            hidden_ref[:, lanes].astype(jnp.float32) * scale * gain[block : block + 1, :]
        ).astype(jnp.bfloat16)
    packed = jnp.dot(selector, hidden_ref[...], preferred_element_type=jnp.float32)
    all_ref[...] = packed.astype(jnp.bfloat16)
    row = lax.broadcasted_iota(jnp.int32, (few, LANES), 0)
    first_ref[:, LANES:] = packed[:few, LANES:].astype(jnp.bfloat16)
    first_ref[:, :LANES] = jnp.where(row == few - 1, code, packed[:few, :LANES]).astype(
        jnp.bfloat16
    )


def pack(hidden, norm_gain, own):
    tokens, features = hidden.shape
    slots = tokens // 2
    few = 3 * slots // 4
    return pl.pallas_call(
        pack_kernel,
        in_specs=[pl.BlockSpec(memory_space=pltpu.HBM)] * 3,
        out_shape=(
            jax.ShapeDtypeStruct((few, features), jnp.bfloat16),
            jax.ShapeDtypeStruct((slots, features), jnp.bfloat16),
            jax.ShapeDtypeStruct((tokens, 1), jnp.int32),
            jax.ShapeDtypeStruct((tokens, 1), jnp.float32),
        ),
        scratch_shapes=[
            VMEM((tokens, features), jnp.bfloat16),
            VMEM((features // LANES, LANES), jnp.bfloat16),
            VMEM((1, tokens), jnp.float32),
            pltpu.SemaphoreType.DMA((3,)),
        ],
        compiler_params=pltpu.CompilerParams(vmem_limit_bytes=16 * 1024 * 1024),
    )(hidden, norm_gain.reshape(features // LANES, LANES), own.reshape(1, tokens))


def rank_kernel(devices, cap_rows, rows_ref, asked_ref, scale_ref, weight_ref, level_ref):
    count = rows_ref.shape[0] // devices
    slots = LANES // 2
    lane = lax.broadcasted_iota(jnp.int32, (1, LANES), 1)
    asked = asked_ref[...]
    ahead = jnp.zeros((asked.shape[0], LANES), jnp.float32)
    held = []
    for device in range(devices):
        tile = rows_ref[pl.ds(device * count + count - 16, 16), :LANES].astype(jnp.float32)
        code = tile[15:16, :]
        whole = jnp.where(lane < slots, code * RADIX + pltpu.roll(code, slots, 1), 2.0 * NO_TOKEN)
        held.append(whole)
        ahead += (whole < asked).astype(jnp.float32)
    rank = jnp.sum(ahead, axis=1, keepdims=True)
    weight_ref[...] = jnp.where((asked < NO_TOKEN) & (rank < cap_rows), as_column(scale_ref[...]), 0.0)
    table = jnp.concatenate(held, axis=0)
    column = lax.broadcasted_iota(jnp.int32, table.shape, 1)
    level = jnp.zeros((devices, 1), jnp.float32)
    for edge in (FEW, count - 1):
        asked = jnp.sum(jnp.where(column == edge, table, 0.0), axis=1, keepdims=True)
        ahead = jnp.zeros((devices, LANES), jnp.float32)
        for whole in held:
            ahead += (whole < asked).astype(jnp.float32)
        rank = jnp.sum(ahead, axis=1, keepdims=True)
        level += jnp.where((asked < NO_TOKEN) & (rank < cap_rows), 1.0, 0.0)
    level_ref[0, 0] = jnp.max(level).astype(jnp.int32)


def ranks(rows, asked, scale, devices, cap_rows):
    return pl.pallas_call(
        functools.partial(rank_kernel, devices, cap_rows),
        in_specs=[pl.BlockSpec(memory_space=VMEM)] * 3,
        out_specs=(
            pl.BlockSpec(memory_space=VMEM),
            pl.BlockSpec(memory_space=pltpu.SMEM),
        ),
        out_shape=(
            jax.ShapeDtypeStruct(asked.shape, jnp.float32),
            jax.ShapeDtypeStruct((1, 1), jnp.int32),
        ),
        compiler_params=pltpu.CompilerParams(vmem_limit_bytes=8 * 1024 * 1024),
    )(rows, asked, scale)


def parts(count, features):
    blocks = features // LANES
    whole = FEW // TILE * TILE
    shared = pl.cdiv(blocks * (FEW - whole), TILE) * TILE
    return blocks * count + SPARE, blocks * whole + shared + SPARE


def down_kernel(
    units_ref, down_ref, level_ref, many_hbm, few_hbm, hidden_ref, many_ref, few_ref, sent
):
    fr_dev, features = down_ref.shape
    devices = sum(BLOCKS)
    count = units_ref.shape[1] // devices
    many_part, few_part = parts(count, features)
    blocks = features // LANES
    whole = FEW // TILE * TILE
    rest = FEW - whole
    few = level_ref[0, 0] == 0

    def multiply(first, held, kept):
        ready = []
        for device in range(first, first + held):
            slots = slice(device * count, device * count + kept)
            gate = units_ref[0, slots, :] * (1.0 / ROW_SCALE)
            up = units_ref[1, slots, :] * (1.0 / ROW_SCALE)
            ready.append(gate * up / (1.0 + jnp.exp(-gate)))
        span = slice(first * kept, (first + held) * kept)
        hidden_ref[span, :] = jnp.concatenate(ready, axis=0).astype(jnp.bfloat16)
        return jnp.dot(hidden_ref[span, :], down_ref[...], preferred_element_type=jnp.float32)

    def clear(ref, start, stop):
        if start < stop:
            ref[start:stop, :] = jnp.zeros((stop - start, LANES), jnp.bfloat16)

    def copy(source, target, device, part):
        span = slice(device * part, min((device + 1) * part, source.shape[0]))
        return pltpu.make_async_copy(source.at[span, :], target.at[span, :], sent.at[device])

    @pl.when(few)
    def _():
        first = 0
        for held in FEW_BLOCKS:
            sums = multiply(first, held, FEW)
            for local in range(held):
                device = first + local
                start = device * few_part
                sum_rows = sums[local * FEW : (local + 1) * FEW, :]
                for block in range(blocks):
                    lanes = slice(block * LANES, (block + 1) * LANES)
                    few_ref[start : start + whole, :] = sum_rows[:whole, lanes].astype(jnp.bfloat16)
                    start += whole
                for block in range(0, blocks, TILE // rest):
                    pieces = [
                        sum_rows[whole:, b * LANES : (b + 1) * LANES]
                        if b < blocks
                        else jnp.zeros((rest, LANES), jnp.float32)
                        for b in range(block, block + TILE // rest)
                    ]
                    few_ref[start : start + TILE, :] = jnp.concatenate(pieces, axis=0).astype(
                        jnp.bfloat16
                    )
                    start += TILE
                clear(few_ref, start, min((device + 1) * few_part, few_ref.shape[0]))
                copy(few_ref, few_hbm, device, few_part).start()
            first += held
        for device in range(devices):
            copy(few_ref, few_hbm, device, few_part).wait()

    @pl.when(jnp.logical_not(few))
    def _():
        first = 0
        for held in BLOCKS:
            sums = multiply(first, held, count)
            for local in range(held):
                device = first + local
                start = device * many_part
                for block in range(blocks):
                    many_ref[start : start + count, :] = sums[
                        local * count : (local + 1) * count, block * LANES : (block + 1) * LANES
                    ].astype(jnp.bfloat16)
                    start += count
                clear(many_ref, start, min((device + 1) * many_part, many_ref.shape[0]))
                copy(many_ref, many_hbm, device, many_part).start()
            first += held
        for device in range(devices):
            copy(many_ref, many_hbm, device, many_part).wait()


def down_shares(units, expert_down, level, devices):
    _, slots, fr_dev = units.shape
    features = expert_down.shape[1]
    shapes = [
        (devices * (part - 1), LANES) for part in parts(slots // devices, features)
    ]
    return pl.pallas_call(
        down_kernel,
        in_specs=[
            pl.BlockSpec(memory_space=VMEM),
            pl.BlockSpec(memory_space=VMEM),
            pl.BlockSpec(memory_space=pltpu.SMEM),
        ],
        out_specs=[pl.BlockSpec(memory_space=pltpu.HBM)] * 2,
        out_shape=[jax.ShapeDtypeStruct(shape, jnp.bfloat16) for shape in shapes],
        scratch_shapes=[
            VMEM((slots, fr_dev), jnp.bfloat16),
            VMEM(shapes[0], jnp.bfloat16),
            VMEM(shapes[1], jnp.bfloat16),
            pltpu.SemaphoreType.DMA((devices,)),
        ],
        compiler_params=pltpu.CompilerParams(vmem_limit_bytes=32 * 1024 * 1024),
        cost_estimate=pl.CostEstimate(
            flops=2 * slots * fr_dev * features,
            bytes_accessed=2 * fr_dev * features + 2 * shapes[0][0] * LANES,
            transcendentals=slots * fr_dev,
        ),
    )(units, expert_down, level)


def expert_units(rows, expert_gate_up):
    return jnp.einsum("td,dgf->gtf", rows, expert_gate_up, preferred_element_type=jnp.float32)


def finish_kernel(
    count, chunk_ref, slot_ref, weight_ref, hidden_ref, out_hbm, rows_ref, out_ref, sent
):
    tokens, features = hidden_ref.shape
    blocks = features // LANES
    whole = count // TILE * TILE
    rest = count - whole
    span = whole + SPARE
    shift = lax.axis_index("sx")
    slot = slot_ref[...]

    def places(width, first, last, start):
        row = lax.broadcasted_iota(jnp.int32, (tokens, width), 1)
        hit = (row == slot - first + start + shift) & (slot >= first) & (slot < last)
        return jnp.where(hit, 1.0, 0.0).astype(jnp.bfloat16)

    def window(start, width, row, lanes):
        rows_ref[row : row + width, lanes] = chunk_ref[start : start + width, :]

    group = TILE // rest if rest else 0
    shared = [places(2 * TILE, whole, count, piece * rest) for piece in range(group)]
    place = jnp.concatenate([places(span, 0, whole, 0)] + shared, axis=1)
    copies = []
    for step in range(features // COLUMNS):
        for block in range(step * COLUMNS // LANES, (step + 1) * COLUMNS // LANES):
            lanes = slice(block * LANES, (block + 1) * LANES)
            window(block * whole, span, 0, lanes)
            for piece in range(group):
                row = span + piece * 2 * TILE
                if piece == block % group:
                    window(blocks * whole + block // group * TILE, 2 * TILE, row, lanes)
                else:
                    rows_ref[row : row + 2 * TILE, lanes] = jnp.zeros((2 * TILE, LANES), jnp.bfloat16)
        lanes = slice(step * COLUMNS, (step + 1) * COLUMNS)
        routed = jnp.dot(place, rows_ref[:, lanes], preferred_element_type=jnp.float32)
        out_ref[:, lanes] = (
            hidden_ref[:, lanes].astype(jnp.float32) + weight_ref[...] * routed
        ).astype(jnp.bfloat16)
        copy = pltpu.make_async_copy(out_ref.at[:, lanes], out_hbm.at[:, lanes], sent.at[step])
        copy.start()
        copies.append(copy)
    for copy in copies:
        copy.wait()


def finish(count, chunk, slot, weight, hidden):
    rest = count % TILE
    rows = count - rest + SPARE + (TILE // rest * 2 * TILE if rest else 0)
    return pl.pallas_call(
        functools.partial(finish_kernel, count),
        in_specs=[pl.BlockSpec(memory_space=VMEM)] * 4,
        out_specs=pl.BlockSpec(memory_space=pltpu.HBM),
        out_shape=jax.ShapeDtypeStruct(hidden.shape, hidden.dtype),
        scratch_shapes=[
            VMEM((rows, hidden.shape[1]), chunk.dtype),
            VMEM(hidden.shape, hidden.dtype),
            pltpu.SemaphoreType.DMA((hidden.shape[1] // COLUMNS,)),
        ],
        compiler_params=pltpu.CompilerParams(vmem_limit_bytes=8 * 1024 * 1024),
    )(chunk, slot, weight, hidden)


def wide_share(rows, expert_gate_up, expert_down, chunk):
    devices, count, features = rows.shape
    fr_dev = expert_down.shape[0]
    normed = rows.reshape(devices * count, features).astype(jnp.bfloat16)
    units = expert_units(normed, expert_gate_up) * (1.0 / ROW_SCALE)
    hidden = (jax.nn.silu(units[0]) * units[1]).astype(jnp.bfloat16)
    hidden = jnp.pad(
        hidden.reshape(devices, count, fr_dev), ((0, 0), (0, chunk - count), (0, 0))
    )
    return jnp.dot(
        hidden.reshape(devices * chunk, fr_dev), expert_down, preferred_element_type=jnp.float32
    ).astype(jnp.bfloat16)


def on_device(hidden, norm_gain, route_expert, route_weight, priority, expert_gate_up, expert_down):
    devices = lax.axis_size("sx")
    tok_dev = hidden.shape[0]
    slot_count = tok_dev // 2
    cap_rows = 3 * slot_count * devices // 8
    own = jnp.where(route_expert[:, 0] == 0, priority, NO_TOKEN).astype(jnp.float32)
    first, every, slot, asked = pack(hidden, norm_gain, own)
    gathered = lax.all_gather(first.astype(jnp.float16), "sx", axis=0, tiled=True)
    rows = lax.optimization_barrier(gathered.astype(jnp.bfloat16))
    weight, level = ranks(rows, asked, route_weight.reshape(1, tok_dev), devices, cap_rows)
    level = level[0, 0]
    index = lax.clamp(jnp.int32(0), level, jnp.int32(2))
    rows, weight, ready = lax.optimization_barrier((rows, weight, index))
    many_share, few_share = down_shares(
        expert_units(rows, expert_gate_up), expert_down, ready.reshape(1, 1), devices
    )

    def few(many_share, few_share, every):
        chunk = lax.psum_scatter(few_share, "sx", scatter_dimension=0, tiled=True)
        return finish(FEW, jnp.pad(chunk, ((0, 1), (0, 0))), slot, weight, hidden)

    def many(many_share, few_share, every):
        chunk = lax.psum_scatter(many_share, "sx", scatter_dimension=0, tiled=True)
        return finish(first.shape[0], jnp.pad(chunk, ((0, 1), (0, 0))), slot, weight, hidden)

    def wide(many_share, few_share, every):
        rows = lax.all_gather(every.astype(jnp.float16), "sx", axis=0, tiled=False)
        share = wide_share(rows, expert_gate_up, expert_down, slot_count + 15)
        returned = lax.psum_scatter(share, "sx", scatter_dimension=0, tiled=True)
        place = (jnp.arange(slot_count + 15, dtype=jnp.int32)[None, :] == slot).astype(jnp.bfloat16)
        routed = jnp.dot(place, returned, preferred_element_type=jnp.float32)
        return (hidden.astype(jnp.float32) + weight * routed).astype(jnp.bfloat16)

    return lax.switch(level, (few, many, wide), many_share, few_share, every)


def solution(mesh):
    in_specs = (
        P(("dp", "sx"), None),
        P(),
        P(("dp", "sx"), None),
        P(("dp", "sx")),
        P(("dp", "sx")),
        P(None, None, "sx"),
        P("sx", None),
    )
    out_specs = P(("dp", "sx"), None)
    return jax.shard_map(
        on_device, mesh=mesh, in_specs=in_specs, out_specs=out_specs, check_vma=False
    )
```

```python
import functools

import jax
import jax.numpy as jnp
from jax import lax
from jax.experimental import pallas as pl
from jax.experimental.pallas import tpu as pltpu
from jax.sharding import PartitionSpec as P

ROW_SCALE = 256.0
NO_TOKEN = 4096
RADIX = 64
LANES = 128
TILE = 16
FEW = 40
COLUMNS = 640
SPARE = TILE
BLOCKS = (6, 6, 4)
FEW_BLOCKS = (7, 6, 3)
VMEM = pltpu.VMEM


def as_column(row):
    n = row.shape[1]
    square = lax.broadcasted_iota(jnp.int32, (n, n), 0) == lax.broadcasted_iota(
        jnp.int32, (n, n), 1
    )
    return jnp.sum(jnp.where(square, row, jnp.zeros_like(row)), axis=1, keepdims=True)


def pack_kernel(
    hidden_hbm, gain_hbm, own_hbm, first_ref, all_ref, slot_ref, asked_ref,
    hidden_ref, gain_ref, own_ref, arrived,
):
    copies = [
        pltpu.make_async_copy(source, target, arrived.at[i])
        for i, (source, target) in enumerate(
            (
                (own_hbm, own_ref),
                (gain_hbm, gain_ref),
                (hidden_hbm, hidden_ref),
            )
        )
    ]
    for copy in copies:
        copy.start()
    for copy in copies[:2]:
        copy.wait()
    slots, features = all_ref.shape
    few = first_ref.shape[0]
    tokens = hidden_ref.shape[0]
    own = own_ref[...]
    own_column = as_column(own)
    slot_row = jnp.sum((own_column < own).astype(jnp.float32), axis=0, keepdims=True)
    slot_column = jnp.sum((own < own_column).astype(jnp.float32), axis=1, keepdims=True)
    slot_row = jnp.where(own < NO_TOKEN, slot_row, float(slots))
    slot_column = jnp.where(own_column < NO_TOKEN, slot_column, float(slots))
    slot_ref[...] = slot_column.astype(jnp.int32)
    asked_ref[...] = own_column
    place = lax.broadcasted_iota(jnp.int32, (slots, tokens), 0).astype(jnp.float32) == slot_row
    selector = jnp.where(place, ROW_SCALE, 0.0).astype(jnp.bfloat16)

    lane = lax.broadcasted_iota(jnp.int32, (tokens, LANES), 1)
    holds = lax.rem(lane, slots).astype(jnp.float32) == slot_column
    held = NO_TOKEN + jnp.sum(
        jnp.where(holds, own_column - NO_TOKEN, 0.0), axis=0, keepdims=True
    )
    quotient = jnp.floor(held * (1.0 / RADIX))
    low = lax.broadcasted_iota(jnp.int32, (1, LANES), 1) < slots
    code = jnp.where(low, quotient, held - quotient * RADIX)

    gain = gain_ref[...].astype(jnp.float32)
    copies[2].wait()
    resid = hidden_ref[...].astype(jnp.float32)
    scale = lax.rsqrt(jnp.mean(resid * resid, axis=1, keepdims=True) + 1e-06)
    for block in range(features // LANES):
        lanes = slice(block * LANES, (block + 1) * LANES)
        hidden_ref[:, lanes] = (
            hidden_ref[:, lanes].astype(jnp.float32) * scale * gain[block : block + 1, :]
        ).astype(jnp.bfloat16)
    packed = jnp.dot(selector, hidden_ref[...], preferred_element_type=jnp.float32)
    all_ref[...] = packed.astype(jnp.bfloat16)
    row = lax.broadcasted_iota(jnp.int32, (few, LANES), 0)
    first_ref[:, LANES:] = packed[:few, LANES:].astype(jnp.bfloat16)
    first_ref[:, :LANES] = jnp.where(row == few - 1, code, packed[:few, :LANES]).astype(
        jnp.bfloat16
    )


def pack(hidden, norm_gain, own):
    tokens, features = hidden.shape
    slots = tokens // 2
    few = 3 * slots // 4
    return pl.pallas_call(
        pack_kernel,
        in_specs=[pl.BlockSpec(memory_space=pltpu.HBM)] * 3,
        out_shape=(
            jax.ShapeDtypeStruct((few, features), jnp.bfloat16),
            jax.ShapeDtypeStruct((slots, features), jnp.bfloat16),
            jax.ShapeDtypeStruct((tokens, 1), jnp.int32),
            jax.ShapeDtypeStruct((tokens, 1), jnp.float32),
        ),
        scratch_shapes=[
            VMEM((tokens, features), jnp.bfloat16),
            VMEM((features // LANES, LANES), jnp.bfloat16),
            VMEM((1, tokens), jnp.float32),
            pltpu.SemaphoreType.DMA((3,)),
        ],
        compiler_params=pltpu.CompilerParams(vmem_limit_bytes=16 * 1024 * 1024),
    )(hidden, norm_gain.reshape(features // LANES, LANES), own.reshape(1, tokens))


def rank_kernel(devices, cap_rows, rows_ref, asked_ref, scale_ref, weight_ref, level_ref):
    count = rows_ref.shape[0] // devices
    slots = LANES // 2
    lane = lax.broadcasted_iota(jnp.int32, (1, LANES), 1)
    asked = asked_ref[...]
    ahead = jnp.zeros((asked.shape[0], LANES), jnp.float32)
    held = []
    for device in range(devices):
        tile = rows_ref[pl.ds(device * count + count - 16, 16), :LANES].astype(jnp.float32)
        code = tile[15:16, :]
        whole = jnp.where(lane < slots, code * RADIX + pltpu.roll(code, slots, 1), 2.0 * NO_TOKEN)
        held.append(whole)
        ahead += (whole < asked).astype(jnp.float32)
    rank = jnp.sum(ahead, axis=1, keepdims=True)
    weight_ref[...] = jnp.where((asked < NO_TOKEN) & (rank < cap_rows), as_column(scale_ref[...]), 0.0)
    table = jnp.concatenate(held, axis=0)
    column = lax.broadcasted_iota(jnp.int32, table.shape, 1)
    level = jnp.zeros((devices, 1), jnp.float32)
    for edge in (FEW, count - 1):
        asked = jnp.sum(jnp.where(column == edge, table, 0.0), axis=1, keepdims=True)
        ahead = jnp.zeros((devices, LANES), jnp.float32)
        for whole in held:
            ahead += (whole < asked).astype(jnp.float32)
        rank = jnp.sum(ahead, axis=1, keepdims=True)
        level += jnp.where((asked < NO_TOKEN) & (rank < cap_rows), 1.0, 0.0)
    level_ref[0, 0] = jnp.max(level).astype(jnp.int32)


def ranks(rows, asked, scale, devices, cap_rows):
    return pl.pallas_call(
        functools.partial(rank_kernel, devices, cap_rows),
        in_specs=[pl.BlockSpec(memory_space=VMEM)] * 3,
        out_specs=(
            pl.BlockSpec(memory_space=VMEM),
            pl.BlockSpec(memory_space=pltpu.SMEM),
        ),
        out_shape=(
            jax.ShapeDtypeStruct(asked.shape, jnp.float32),
            jax.ShapeDtypeStruct((1, 1), jnp.int32),
        ),
        compiler_params=pltpu.CompilerParams(vmem_limit_bytes=8 * 1024 * 1024),
    )(rows, asked, scale)


def parts(count, features):
    blocks = features // LANES
    whole = FEW // TILE * TILE
    shared = pl.cdiv(blocks * (FEW - whole), TILE) * TILE
    return blocks * count + SPARE, blocks * whole + shared + SPARE


def down_kernel(
    units_ref, down_ref, level_ref, many_hbm, few_hbm, hidden_ref, many_ref, few_ref, sent
):
    fr_dev, features = down_ref.shape
    devices = sum(BLOCKS)
    count = units_ref.shape[1] // devices
    many_part, few_part = parts(count, features)
    blocks = features // LANES
    whole = FEW // TILE * TILE
    rest = FEW - whole
    few = level_ref[0, 0] == 0

    def multiply(first, held, kept):
        ready = []
        for device in range(first, first + held):
            slots = slice(device * count, device * count + kept)
            gate = units_ref[0, slots, :] * (1.0 / ROW_SCALE)
            up = units_ref[1, slots, :] * (1.0 / ROW_SCALE)
            ready.append(gate * up / (1.0 + jnp.exp(-gate)))
        span = slice(first * kept, (first + held) * kept)
        hidden_ref[span, :] = jnp.concatenate(ready, axis=0).astype(jnp.bfloat16)
        return jnp.dot(hidden_ref[span, :], down_ref[...], preferred_element_type=jnp.float32)

    def clear(ref, start, stop):
        if start < stop:
            ref[start:stop, :] = jnp.zeros((stop - start, LANES), jnp.bfloat16)

    def copy(source, target, device, part):
        span = slice(device * part, min((device + 1) * part, source.shape[0]))
        return pltpu.make_async_copy(source.at[span, :], target.at[span, :], sent.at[device])

    @pl.when(few)
    def _():
        first = 0
        for held in FEW_BLOCKS:
            sums = multiply(first, held, FEW)
            for local in range(held):
                device = first + local
                start = device * few_part
                sum_rows = sums[local * FEW : (local + 1) * FEW, :]
                for block in range(blocks):
                    lanes = slice(block * LANES, (block + 1) * LANES)
                    few_ref[start : start + whole, :] = sum_rows[:whole, lanes].astype(jnp.bfloat16)
                    start += whole
                for block in range(0, blocks, TILE // rest):
                    pieces = [
                        sum_rows[whole:, b * LANES : (b + 1) * LANES]
                        if b < blocks
                        else jnp.zeros((rest, LANES), jnp.float32)
                        for b in range(block, block + TILE // rest)
                    ]
                    few_ref[start : start + TILE, :] = jnp.concatenate(pieces, axis=0).astype(
                        jnp.bfloat16
                    )
                    start += TILE
                clear(few_ref, start, min((device + 1) * few_part, few_ref.shape[0]))
                copy(few_ref, few_hbm, device, few_part).start()
            first += held
        for device in range(devices):
            copy(few_ref, few_hbm, device, few_part).wait()

    @pl.when(jnp.logical_not(few))
    def _():
        first = 0
        for held in BLOCKS:
            sums = multiply(first, held, count)
            for local in range(held):
                device = first + local
                start = device * many_part
                for block in range(blocks):
                    many_ref[start : start + count, :] = sums[
                        local * count : (local + 1) * count, block * LANES : (block + 1) * LANES
                    ].astype(jnp.bfloat16)
                    start += count
                clear(many_ref, start, min((device + 1) * many_part, many_ref.shape[0]))
                copy(many_ref, many_hbm, device, many_part).start()
            first += held
        for device in range(devices):
            copy(many_ref, many_hbm, device, many_part).wait()


def down_shares(units, expert_down, level, devices):
    _, slots, fr_dev = units.shape
    features = expert_down.shape[1]
    shapes = [
        (devices * (part - 1), LANES) for part in parts(slots // devices, features)
    ]
    return pl.pallas_call(
        down_kernel,
        in_specs=[
            pl.BlockSpec(memory_space=VMEM),
            pl.BlockSpec(memory_space=VMEM),
            pl.BlockSpec(memory_space=pltpu.SMEM),
        ],
        out_specs=[pl.BlockSpec(memory_space=pltpu.HBM)] * 2,
        out_shape=[jax.ShapeDtypeStruct(shape, jnp.bfloat16) for shape in shapes],
        scratch_shapes=[
            VMEM((slots, fr_dev), jnp.bfloat16),
            VMEM(shapes[0], jnp.bfloat16),
            VMEM(shapes[1], jnp.bfloat16),
            pltpu.SemaphoreType.DMA((devices,)),
        ],
        compiler_params=pltpu.CompilerParams(vmem_limit_bytes=32 * 1024 * 1024),
        cost_estimate=pl.CostEstimate(
            flops=2 * slots * fr_dev * features,
            bytes_accessed=2 * fr_dev * features + 2 * shapes[0][0] * LANES,
            transcendentals=slots * fr_dev,
        ),
    )(units, expert_down, level)


def expert_units(rows, expert_gate_up):
    return jnp.einsum("td,dgf->gtf", rows, expert_gate_up, preferred_element_type=jnp.float32)


def finish_kernel(
    count, chunk_ref, slot_ref, weight_ref, hidden_ref, out_hbm, rows_ref, out_ref, sent
):
    tokens, features = hidden_ref.shape
    blocks = features // LANES
    whole = count // TILE * TILE
    rest = count - whole
    span = whole + SPARE
    shift = lax.axis_index("sx")
    slot = slot_ref[...]

    def places(width, first, last, start):
        row = lax.broadcasted_iota(jnp.int32, (tokens, width), 1)
        hit = (row == slot - first + start + shift) & (slot >= first) & (slot < last)
        return jnp.where(hit, 1.0, 0.0).astype(jnp.bfloat16)

    def window(start, width, row, lanes):
        rows_ref[row : row + width, lanes] = chunk_ref[start : start + width, :]

    group = TILE // rest if rest else 0
    shared = [places(2 * TILE, whole, count, piece * rest) for piece in range(group)]
    place = jnp.concatenate([places(span, 0, whole, 0)] + shared, axis=1)
    copies = []
    for step in range(features // COLUMNS):
        for block in range(step * COLUMNS // LANES, (step + 1) * COLUMNS // LANES):
            lanes = slice(block * LANES, (block + 1) * LANES)
            window(block * whole, span, 0, lanes)
            for piece in range(group):
                row = span + piece * 2 * TILE
                if piece == block % group:
                    window(blocks * whole + block // group * TILE, 2 * TILE, row, lanes)
                else:
                    rows_ref[row : row + 2 * TILE, lanes] = jnp.zeros((2 * TILE, LANES), jnp.bfloat16)
        lanes = slice(step * COLUMNS, (step + 1) * COLUMNS)
        routed = jnp.dot(place, rows_ref[:, lanes], preferred_element_type=jnp.float32)
        out_ref[:, lanes] = (
            hidden_ref[:, lanes].astype(jnp.float32) + weight_ref[...] * routed
        ).astype(jnp.bfloat16)
        copy = pltpu.make_async_copy(out_ref.at[:, lanes], out_hbm.at[:, lanes], sent.at[step])
        copy.start()
        copies.append(copy)
    for copy in copies:
        copy.wait()


def finish(count, chunk, slot, weight, hidden):
    rest = count % TILE
    rows = count - rest + SPARE + (TILE // rest * 2 * TILE if rest else 0)
    return pl.pallas_call(
        functools.partial(finish_kernel, count),
        in_specs=[pl.BlockSpec(memory_space=VMEM)] * 4,
        out_specs=pl.BlockSpec(memory_space=pltpu.HBM),
        out_shape=jax.ShapeDtypeStruct(hidden.shape, hidden.dtype),
        scratch_shapes=[
            VMEM((rows, hidden.shape[1]), chunk.dtype),
            VMEM(hidden.shape, hidden.dtype),
            pltpu.SemaphoreType.DMA((hidden.shape[1] // COLUMNS,)),
        ],
        compiler_params=pltpu.CompilerParams(vmem_limit_bytes=8 * 1024 * 1024),
    )(chunk, slot, weight, hidden)


def wide_share(rows, expert_gate_up, expert_down, chunk):
    devices, count, features = rows.shape
    fr_dev = expert_down.shape[0]
    normed = rows.reshape(devices * count, features).astype(jnp.bfloat16)
    units = expert_units(normed, expert_gate_up) * (1.0 / ROW_SCALE)
    hidden = (jax.nn.silu(units[0]) * units[1]).astype(jnp.bfloat16)
    hidden = jnp.pad(
        hidden.reshape(devices, count, fr_dev), ((0, 0), (0, chunk - count), (0, 0))
    )
    return jnp.dot(
        hidden.reshape(devices * chunk, fr_dev), expert_down, preferred_element_type=jnp.float32
    ).astype(jnp.bfloat16)


def on_device(hidden, norm_gain, route_expert, route_weight, priority, expert_gate_up, expert_down):
    devices = lax.axis_size("sx")
    tok_dev = hidden.shape[0]
    slot_count = tok_dev // 2
    cap_rows = 3 * slot_count * devices // 8
    own = jnp.where(route_expert[:, 0] == 0, priority, NO_TOKEN).astype(jnp.float32)
    first, every, slot, asked = pack(hidden, norm_gain, own)
    gathered = lax.all_gather(first.astype(jnp.float16), "sx", axis=0, tiled=True)
    rows = lax.optimization_barrier(gathered.astype(jnp.bfloat16))
    weight, level = ranks(rows, asked, route_weight.reshape(1, tok_dev), devices, cap_rows)
    level = level[0, 0]
    index = lax.clamp(jnp.int32(0), level, jnp.int32(2))
    rows, weight, ready = lax.optimization_barrier((rows, weight, index))
    many_share, few_share = down_shares(
        expert_units(rows, expert_gate_up), expert_down, ready.reshape(1, 1), devices
    )

    def few(many_share, few_share, every):
        chunk = lax.psum_scatter(few_share, "sx", scatter_dimension=0, tiled=True)
        return finish(FEW, jnp.pad(chunk, ((0, 1), (0, 0))), slot, weight, hidden)

    def many(many_share, few_share, every):
        chunk = lax.psum_scatter(many_share, "sx", scatter_dimension=0, tiled=True)
        return finish(first.shape[0], jnp.pad(chunk, ((0, 1), (0, 0))), slot, weight, hidden)

    def wide(many_share, few_share, every):
        rows = lax.all_gather(every.astype(jnp.float16), "sx", axis=0, tiled=False)
        share = wide_share(rows, expert_gate_up, expert_down, slot_count + 15)
        returned = lax.psum_scatter(share, "sx", scatter_dimension=0, tiled=True)
        place = (jnp.arange(slot_count + 15, dtype=jnp.int32)[None, :] == slot).astype(jnp.bfloat16)
        routed = jnp.dot(place, returned, preferred_element_type=jnp.float32)
        return (hidden.astype(jnp.float32) + weight * routed).astype(jnp.bfloat16)

    return lax.switch(level, (few, many, wide), many_share, few_share, every)


def solution(mesh):
    in_specs = (
        P(("dp", "sx"), None),
        P(),
        P(("dp", "sx"), None),
        P(("dp", "sx")),
        P(("dp", "sx")),
        P(None, None, "sx"),
        P("sx", None),
    )
    out_specs = P(("dp", "sx"), None)
    return jax.shard_map(
        on_device, mesh=mesh, in_specs=in_specs, out_specs=out_specs, check_vma=False
    )
```
